256 devices in a mesh: ctx: 32 (over z, x), tp: 4 (over y), dp: 2 (over core).
Axes of the slice: x: 4, y: 4, z: 8, core: 2. Of those that a mesh axis runs over, the one named last changes fastest.
Arguments:
- queries: bfloat16 [16384, 4096], P(('dp', 'ctx'), 'tp'), parts along dimension 0, may hold values from -12 to 12
- keys: bfloat16 [16384, 512], P(('dp', 'ctx'), 'tp'), parts along dimension 0, may hold values from -6 to 6
- values: bfloat16 [16384, 512], P(('dp', 'ctx'), 'tp'), parts along dimension 0, may hold values from -6 to 6
- out_weight: bfloat16 [4096, 4096], P('tp'), may hold values from -0.75 to 0.75
- doc_ids: int32 [16384], P(('dp', 'ctx')), parts along dimension 0, may hold values from 0 to 8191, as said below
Outputs:
- projected: bfloat16 [16384, 4096], P(('dp', 'ctx'), 'tp'), parts along dimension 0
The draws below stay inside these ranges and needn't reach their ends.
There are 2 independent parts, one for each index of `dp`. The reference program is written for one: setup_inputs(seed, part) draws one part's arguments, and reference() takes and returns one part's arrays. A program takes and returns all parts, laid end to end along the dimension named above; an argument that names none is the same for every part. Nothing has to cross between parts.
Inputs may be any that keep to these rules, and one draw needn't show every extreme that they name: `doc_ids`: ids never fall along the sequence; a document's id is the position of its first token; a document holds at most 4096 tokens, the second document holds exactly 4096, and the last token is a document of its own.
All inputs are finite; a program needn't handle non-finite values.
Results may differ from the reference program's by a relative error of at most 0.014.
Values may be sent and summed in bfloat16 or wider, within the bound.
A program may use at most 128 MiB of HBM per device.

```python
import jax
import jax.numpy as jnp
from jax import lax

HEAD_SIZE = 128
QUERY_HEAD_COUNT = 32
KEY_VALUE_HEADS = 4
D = 4096
TOKENS_PER_SHARD = 256
DOC_MOST = 4096
PACKED_TOKENS = 8192
N_TP = 4


def doc_starts(key):
    key = jax.random.fold_in(key, 101)
    position = jnp.arange(PACKED_TOKENS, dtype=jnp.int32)
    offset = TOKENS_PER_SHARD // 2
    within = (position + DOC_MOST - offset) % DOC_MOST
    coin_flips = jax.random.randint(key, (PACKED_TOKENS,), 0, max(TOKENS_PER_SHARD // 2, 2)) == 0
    cut_zone = position >= offset + DOC_MOST
    return (position == 0) | (within == 0) | coin_flips & cut_zone | (position == PACKED_TOKENS - 1)


def draw_doc_ids(key, part):
    starts = doc_starts(key)
    position = jnp.arange(PACKED_TOKENS, dtype=jnp.int32)
    marked = jnp.where(starts, position, jnp.zeros_like(position)).astype(jnp.int32)
    return lax.cummax(marked, axis=0).astype(jnp.int32)


def draw_queries(key, part):
    key = jax.random.fold_in(key, 1)
    backdrop_level = 2.0 * jnp.clip(jax.random.normal(key, (PACKED_TOKENS, QUERY_HEAD_COUNT * HEAD_SIZE), jnp.float32), -6.0, 6.0)
    return backdrop_level.astype(jnp.bfloat16)


def draw_keys(key, part):
    key = jax.random.fold_in(key, 2)
    backdrop_level = jnp.clip(jax.random.normal(key, (PACKED_TOKENS, KEY_VALUE_HEADS * HEAD_SIZE), jnp.float32), -6.0, 6.0)
    return backdrop_level.astype(jnp.bfloat16)


def block_levels(own_key, dims, cuts, least, high):
    loudness, own = 1.0, jax.random.fold_in(own_key, 6)
    for dim, shards_of in cuts:
        steps = jnp.exp(jax.random.uniform(jax.random.fold_in(own, dim), (shards_of,), jnp.float32, least / len(cuts), high / len(cuts)))
        loudness = loudness * jnp.repeat(steps, dims[dim] // shards_of).reshape([-1 if axis == dim else 1 for axis in range(len(dims))])
    return loudness


def noise(stream_key, shape, scale, most, pieces=(), kind=jnp.bfloat16):
    factor_of = block_levels(stream_key, shape, pieces, -0.22, 0.18) if pieces else 1.0
    entries = jax.random.normal(stream_key, shape, jnp.float32) * scale * factor_of
    return jnp.minimum(jnp.maximum(entries, -most), most).astype(kind)


def setup_inputs(seed: int = 0, part: int = 0) -> dict:
    seeds = jax.random.split(jax.random.key(seed), 6)
    own_keys = jax.random.split(jax.random.fold_in(seeds[5], part), 6)
    queries = draw_queries(jax.random.fold_in(jax.random.fold_in(seeds[5], part), 71), part)
    keys = draw_keys(jax.random.fold_in(jax.random.fold_in(seeds[5], part), 71), part)
    values = noise(own_keys[2], (PACKED_TOKENS, KEY_VALUE_HEADS * HEAD_SIZE), 1.0, 6.0, ((0, 32), (1, 4)))
    out_weight = noise(seeds[3], (QUERY_HEAD_COUNT * HEAD_SIZE, D), (QUERY_HEAD_COUNT * HEAD_SIZE // 64) ** -0.5, 0.75, ((0, 4),))
    doc_ids = draw_doc_ids(jax.random.fold_in(jax.random.fold_in(seeds[5], part), 71), part)
    return dict(queries=queries, keys=keys, values=values, out_weight=out_weight, doc_ids=doc_ids)


def reference(queries, keys, values, out_weight, doc_ids):
    group_width = QUERY_HEAD_COUNT // KEY_VALUE_HEADS
    score_scale = 1.0 / (HEAD_SIZE ** 0.5)
    leading_rows = DOC_MOST
    padded_key_rows = jnp.concatenate([jnp.zeros((leading_rows, KEY_VALUE_HEADS * HEAD_SIZE), jnp.bfloat16), keys], axis=0)
    padded_value_rows = jnp.concatenate([jnp.zeros((leading_rows, KEY_VALUE_HEADS * HEAD_SIZE), jnp.bfloat16), values], axis=0)
    docs_padded = jnp.concatenate([jnp.full((leading_rows,), -1, jnp.int32), doc_ids.astype(jnp.int32)], axis=0)
    where_padded = jnp.arange(PACKED_TOKENS + leading_rows, dtype=jnp.int32) - leading_rows
    visible_extent = leading_rows + TOKENS_PER_SHARD

    def query_block(block_index):
        first_row_index = (block_index * TOKENS_PER_SHARD).astype(jnp.int32)
        query_matrix = lax.dynamic_slice_in_dim(queries, first_row_index, TOKENS_PER_SHARD, 0)
        query_matrix = query_matrix.reshape(TOKENS_PER_SHARD, KEY_VALUE_HEADS, group_width, HEAD_SIZE).astype(jnp.float32)
        query_docs = lax.dynamic_slice_in_dim(doc_ids.astype(jnp.int32), first_row_index, TOKENS_PER_SHARD, 0)
        query_where = first_row_index + jnp.arange(TOKENS_PER_SHARD, dtype=jnp.int32)
        key_matrix = lax.dynamic_slice_in_dim(padded_key_rows, first_row_index, visible_extent, 0).reshape(visible_extent, KEY_VALUE_HEADS, HEAD_SIZE).astype(jnp.float32)
        value_matrix = lax.dynamic_slice_in_dim(padded_value_rows, first_row_index, visible_extent, 0).reshape(visible_extent, KEY_VALUE_HEADS, HEAD_SIZE).astype(jnp.float32)
        key_docs = lax.dynamic_slice_in_dim(docs_padded, first_row_index, visible_extent, 0)
        key_where = lax.dynamic_slice_in_dim(where_padded, first_row_index, visible_extent, 0)
        scores = jnp.einsum("qgrd,kgd->grqk", query_matrix, key_matrix) * score_scale
        allowed = (key_docs[None, :] == query_docs[:, None]) & (key_where[None, :] <= query_where[:, None])
        masked = jnp.where(allowed, scores, jnp.float32(-1.0e30))
        row_max = jnp.max(masked, axis=-1)
        weights = jnp.where(allowed, jnp.exp(masked - row_max[..., None]), jnp.float32(0.0))
        totals = jnp.sum(weights, axis=-1)
        rounded_weights = lax.optimization_barrier(weights.astype(jnp.bfloat16)).astype(jnp.float32)
        summed = jnp.einsum("grqk,kgd->grqd", rounded_weights, value_matrix)
        attended = (summed / totals[..., None]).astype(jnp.bfloat16)
        return jnp.transpose(attended, (2, 0, 1, 3)).reshape(TOKENS_PER_SHARD, QUERY_HEAD_COUNT * HEAD_SIZE)

    blocks = lax.map(query_block, jnp.arange(PACKED_TOKENS // TOKENS_PER_SHARD, dtype=jnp.int32))
    attended = blocks.reshape(PACKED_TOKENS, QUERY_HEAD_COUNT * HEAD_SIZE)
    group_cols = QUERY_HEAD_COUNT * HEAD_SIZE // N_TP
    total = jnp.zeros((PACKED_TOKENS, D), jnp.float32)
    for group_index in range(N_TP):
        lower = group_index * group_cols
        partial_g = jnp.dot(attended[:, lower:lower + group_cols], out_weight[lower:lower + group_cols], preferred_element_type=jnp.float32).astype(jnp.bfloat16)
        partial_g = lax.optimization_barrier(partial_g)
        total = total + partial_g.astype(jnp.float32)
    return total.astype(jnp.bfloat16)
```

```python
import functools
import math

import jax
import jax.numpy as jnp
from jax import lax
from jax.experimental import pallas as pl
from jax.experimental.pallas import tpu as pltpu
from jax.sharding import PartitionSpec as P

MESH = pl.DeviceIdType.MESH
TOK = 256
HEADS = 8
HD = 128
NX = 4
NZ = 8
ROW = NX * TOK
OUT = 4096
MINE = 1024
HALF = MINE // 2
CHUNKS = 2
CR = TOK // CHUNKS
LOG2E_SCALE = math.log2(math.e) / math.sqrt(HD)
NEG = -1e30
K, V = 0, 1


def kernel(
    q_hbm, k_hbm, v_hbm, w_hbm, d_ref, out_ref,
    qv, kst, kt, vb, kx, vx, dB, acc, mrow, att, wv,
    snd_a, rcv_a, snd_n, rcv_n,
    lsem, wsem, gs, gr, ds, dr,
):
    ctx = lax.axis_index("ctx")
    y = lax.axis_index("tp")
    z, x = ctx // NX, ctx % NX
    xp, xm, xo = (x + 1) % NX, (x + NX - 1) % NX, (x + 2) % NX
    dev_xp, dev_xm, dev_xo = z * NX + xp, z * NX + xm, z * NX + xo
    dev_zp = ((z + 1) % NZ) * NX + x
    dev_zm = ((z + NZ - 1) % NZ) * NX + x
    yp, ym, yo = (y + 1) % 4, (y + 3) % 4, (y + 2) % 4

    kcp = pltpu.make_async_copy(k_hbm, kst, lsem.at[0])
    vcp = pltpu.make_async_copy(v_hbm, vb.at[0, x], lsem.at[1])
    kcp.start()
    vcp.start()
    barrier = pltpu.get_barrier_semaphore()
    for dev in (dev_xp, dev_xm, dev_xo, dev_zp, dev_zm):
        pl.semaphore_signal(barrier, inc=1, device_id={"ctx": dev}, device_id_type=MESH)
    for dev in (yp, ym):
        pl.semaphore_signal(barrier, inc=1, device_id={"tp": dev}, device_id_type=MESH)
    qcp = []
    for h in range(HEADS):
        cp = pltpu.make_async_copy(q_hbm.at[:, pl.ds(h * HD, HD)], qv.at[h], lsem.at[2 + h])
        cp.start()
        qcp.append(cp)
    wcp = []
    for i in range(4):
        cp = pltpu.make_async_copy(w_hbm.at[pl.ds(i * 256, 256)], wv.at[pl.ds(i * 256, 256)], wsem.at[i])
        cp.start()
        wcp.append(cp)
    dB[...] = jnp.broadcast_to(d_ref[...], (128, TOK)).T
    acc[...] = jnp.zeros_like(acc)
    mrow[...] = jnp.full_like(mrow, NEG)
    kcp.wait()
    kt[0, x] = kst[...].T
    vcp.wait()
    pl.semaphore_wait(barrier, 7)

    pending = []

    def buf(row, col, what):
        if row == 4:
            return (kx, vx)[what]
        return (kt, vb)[what].at[row, col]

    def send(row, col, to_row, dev, whats=(K, V), when=None):
        for what in whats:
            sem = gs.at[len(pending)]
            cp = pltpu.make_async_remote_copy(
                src_ref=buf(row, col, what),
                dst_ref=buf(to_row, col, what),
                send_sem=sem,
                recv_sem=gr.at[to_row, 0 if to_row == 4 else col, what],
                device_id={"ctx": dev},
                device_id_type=MESH,
            )
            pending.append((cp, when))
            if when is None:
                cp.start()
            else:
                pl.when(when)(cp.start)

    def await_block(row, col, whats=(K, V), when=None):
        for what in whats:
            ref = buf(row, col, what)
            cp = pltpu.make_async_copy(ref, ref, gr.at[row, 0 if row == 4 else col, what])
            if when is None:
                cp.wait()
            else:
                pl.when(when)(cp.wait)

    send(0, x, 1, dev_zp)
    send(0, x, 0, dev_xp, when=x < 3)
    send(0, x, 0, dev_xm, when=x == 0)
    send(0, x, 0, dev_xo, whats=(V,), when=x == 1)
    mid = (x == 1) | (x == 2)
    await_block(0, xm, whats=(K,), when=mid)
    send(0, xm, 0, dev_xp, whats=(K,), when=mid)
    await_block(0, xp, whats=(V,), when=x == 3)
    send(0, xp, 0, dev_xm, whats=(V,), when=x == 3)

    def take_column(row):
        await_block(row, x)
        send(row, x, row + 1, dev_zp)
        send(row, x, row, dev_xp)
        send(row, x, row, dev_xm)

    def plane_step(row, lo, hi):
        kcat = jnp.concatenate([kt[row, c] for c in range(NX)], axis=1)
        vcat = vb[row].reshape(ROW, HD)
        vext = jnp.concatenate([vcat, jnp.ones_like(vcat)], axis=1)
        kpos = lax.broadcasted_iota(jnp.int32, (TOK, ROW), 1) + (z - row) * ROW
        allowed = kpos >= jnp.concatenate([dB[...]] * (ROW // 128), axis=1)

        def head(h, carry):
            update(h, slice(None), kcat, vext, allowed)
            return carry

        lax.fori_loop(lo, hi, head, 0)

    def update(h, rows, kcat, vext, allowed):
        s = jnp.dot(qv[h, rows], kcat, preferred_element_type=jnp.float32)
        s = jnp.where(allowed, s, NEG)
        old = mrow[h, rows]
        new = jnp.maximum(old, jnp.max(s, axis=1, keepdims=True))
        p = jnp.exp2((s - jnp.concatenate([new] * (s.shape[1] // 128), axis=1)) * LOG2E_SCALE)
        factor = jnp.exp2((old - new) * LOG2E_SCALE)
        acc[h, rows] = acc[h, rows] * jnp.concatenate([factor, factor], axis=1) + jnp.dot(
            p.astype(jnp.bfloat16), vext, preferred_element_type=jnp.float32
        )
        mrow[h, rows] = new

    take_column(1)
    await_block(1, xm)
    send(1, xm, 1, dev_xp)
    for cp in qcp:
        cp.wait()
    take_column(2)
    await_block(1, xp)
    await_block(1, xo)
    send(1, xo, 2, dev_zp)
    plane_step(1, 0, 4)
    take_column(3)
    plane_step(1, 4, 8)
    await_block(2, xo)
    send(2, xo, 3, dev_zp)
    await_block(2, xp)
    await_block(2, xm)
    plane_step(2, 0, 4)
    await_block(4, x)

    def send4(dev, whats, when):
        for what in whats:
            cp = pltpu.make_async_remote_copy(
                src_ref=buf(4, x, what),
                dst_ref=buf(0, x, what),
                send_sem=gs.at[len(pending)],
                recv_sem=gr.at[0, x, what],
                device_id={"ctx": dev},
                device_id_type=MESH,
            )
            pending.append((cp, when))
            pl.when(when)(cp.start)

    send4(dev_xm, (K, V), x > 0)
    send4(dev_xp, (K, V), x == 3)
    send4(dev_xo, (K,), x == 2)
    plane_step(2, 4, 8)
    await_block(3, xp)
    await_block(3, xm)
    await_block(3, xo)
    await_block(0, xp, whats=(V,), when=mid)
    send(0, xp, 0, dev_xm, whats=(V,), when=mid)
    await_block(0, xm, whats=(K,), when=x == 0)
    send(0, xm, 0, dev_xp, whats=(K,), when=x == 0)
    plane_step(3, 0, 8)

    await_block(0, xm, whats=(K,), when=x == 3)
    await_block(0, xm, whats=(V,))
    await_block(0, xp, whats=(K,))
    await_block(0, xp, whats=(V,), when=x == 0)
    await_block(0, xo)
    for cp in wcp:
        cp.wait()

    def rs_copy(c, slot, src, dst, dev):
        return pltpu.make_async_remote_copy(
            src_ref=src,
            dst_ref=dst,
            send_sem=ds.at[c, slot],
            recv_sem=dr.at[c, slot],
            device_id={"tp": dev},
            device_id_type=MESH,
        )

    def copies(c):
        return (
            rs_copy(c, 0, snd_a.at[c, 0], rcv_a.at[c, 0], yp),
            rs_copy(c, 1, snd_a.at[c, 1], rcv_a.at[c, 1], ym),
            rs_copy(c, 2, snd_n.at[c, 0], rcv_n.at[c, 0], yp),
            rs_copy(c, 3, snd_n.at[c, 1], rcv_n.at[c, 1], ym),
            rs_copy(c, 4, snd_n.at[c, 2], rcv_n.at[c, 2], yp),
            rs_copy(c, 5, snd_n.at[c, 3], rcv_n.at[c, 3], ym),
        )

    def project(c, dest, half):
        cols = pl.ds(pl.multiple_of(dest * MINE + half * HALF, HALF), HALF)
        return jnp.dot(att[c], wv[:, cols], preferred_element_type=jnp.float32)

    lane = lax.broadcasted_iota(jnp.int32, (CR, ROW), 1)
    own_pos = lane + z * ROW - jnp.where(lane // TOK > x, 4 * ROW, 0)
    ext_lane = lax.broadcasted_iota(jnp.int32, (CR, TOK), 1)
    last_pos = jnp.concatenate([own_pos, ext_lane + ((z - 4) * ROW + x * TOK)], axis=1)
    row_at = lax.broadcasted_iota(jnp.int32, (CR, ROW + TOK), 0) + ctx * TOK

    def finish(c, carry):
        rows = pl.ds(pl.multiple_of(c * CR, CR), CR)
        kcat = jnp.concatenate([kt[0, i] for i in range(NX)] + [kx[...]], axis=1)
        vcat = jnp.concatenate([vb[0].reshape(ROW, HD), vx[...]], axis=0)
        vext = jnp.concatenate([vcat, jnp.ones_like(vcat)], axis=1)
        first = jnp.concatenate([dB[rows]] * ((ROW + TOK) // 128), axis=1)
        allowed = (last_pos >= first) & (last_pos <= row_at + c * CR)

        def head(h, carry):
            update(h, rows, kcat, vext, allowed)
            a = acc[h, rows]
            att[c, :, pl.ds(pl.multiple_of(h * HD, HD), HD)] = (a[:, :HD] / a[:, HD:]).astype(jnp.bfloat16)
            return carry

        lax.fori_loop(0, HEADS, head, 0)
        cps = copies(c)
        for i, (dest, half, buffer, slot) in enumerate(
            ((yo, 0, snd_a, 0), (yo, 1, snd_a, 1), (yp, 1, snd_n, 0), (ym, 0, snd_n, 1))
        ):
            buffer[c, slot] = project(c, dest, half).astype(jnp.bfloat16)
            cps[i].start()
        return carry

    lax.fori_loop(0, CHUNKS, finish, 0)

    def relay(c, carry):
        cps = copies(c)
        for i, (dest, half) in enumerate(((yp, 0), (ym, 1))):
            part = project(c, dest, half)
            cps[i].wait_recv()
            snd_n[c, 2 + i] = (part + rcv_a[c, i].astype(jnp.float32)).astype(jnp.bfloat16)
            cps[4 + i].start()
        return carry

    lax.fori_loop(0, CHUNKS, relay, 0)

    def collect(c, carry):
        rows = pl.ds(pl.multiple_of(c * CR, CR), CR)
        cps = copies(c)
        own = [project(c, y, half) for half in (0, 1)]
        for i in range(2, 6):
            cps[i].wait_recv()
        out_ref[rows, :HALF] = (
            own[0] + rcv_n[c, 2].astype(jnp.float32) + rcv_n[c, 1].astype(jnp.float32)
        ).astype(jnp.bfloat16)
        out_ref[rows, HALF:] = (
            own[1] + rcv_n[c, 0].astype(jnp.float32) + rcv_n[c, 3].astype(jnp.float32)
        ).astype(jnp.bfloat16)
        for cp in cps:
            cp.wait_send()
        return carry

    lax.fori_loop(0, CHUNKS, collect, 0)
    for cp, when in pending:
        if when is None:
            cp.wait_send()
        else:
            pl.when(when)(cp.wait_send)


def body(queries, keys, values, out_weight, doc_ids):
    bf, f32 = jnp.bfloat16, jnp.float32
    any_spec = pl.BlockSpec(memory_space=pl.ANY)
    vmem = pl.BlockSpec(memory_space=pltpu.VMEM)
    return pl.pallas_call(
        kernel,
        out_shape=jax.ShapeDtypeStruct((TOK, MINE), bf),
        in_specs=[any_spec] * 4 + [vmem],
        out_specs=vmem,
        scratch_shapes=[
            pltpu.VMEM((HEADS, TOK, HD), bf),
            pltpu.VMEM((TOK, HD), bf),
            pltpu.VMEM((4, NX, HD, TOK), bf),
            pltpu.VMEM((4, NX, TOK, HD), bf),
            pltpu.VMEM((HD, TOK), bf),
            pltpu.VMEM((TOK, HD), bf),
            pltpu.VMEM((TOK, 128), jnp.int32),
            pltpu.VMEM((HEADS, TOK, 2 * HD), f32),
            pltpu.VMEM((HEADS, TOK, 128), f32),
            pltpu.VMEM((CHUNKS, CR, HEADS * HD), bf),
            pltpu.VMEM((HEADS * HD, OUT), bf),
            pltpu.VMEM((CHUNKS, 2, CR, HALF), bf),
            pltpu.VMEM((CHUNKS, 2, CR, HALF), bf),
            pltpu.VMEM((CHUNKS, 4, CR, HALF), bf),
            pltpu.VMEM((CHUNKS, 4, CR, HALF), bf),
            pltpu.SemaphoreType.DMA((2 + HEADS,)),
            pltpu.SemaphoreType.DMA((4,)),
            pltpu.SemaphoreType.DMA((64,)),
            pltpu.SemaphoreType.DMA((5, NX, 2)),
            pltpu.SemaphoreType.DMA((CHUNKS, 6)),
            pltpu.SemaphoreType.DMA((CHUNKS, 6)),
        ],
        compiler_params=pltpu.CompilerParams(
            collective_id=0, has_side_effects=True, vmem_limit_bytes=48 << 20
        ),
        cost_estimate=pl.CostEstimate(flops=7 * 10**9, bytes_accessed=10**7, transcendentals=9 * 10**6),
    )(queries, keys, values, out_weight, doc_ids.reshape(1, TOK))


def solution(mesh):
    placed = (
        P(("dp", "ctx"), "tp"),
        P(("dp", "ctx"), "tp"),
        P(("dp", "ctx"), "tp"),
        P("tp", None),
        P(("dp", "ctx")),
    )
    return jax.shard_map(
        body, mesh=mesh, in_specs=placed, out_specs=P(("dp", "ctx"), "tp"), check_vma=False
    )
```

```python
import math

import jax
import jax.numpy as jnp
from jax import lax
from jax.experimental import pallas as pl
from jax.experimental.pallas import tpu as pltpu
from jax.sharding import PartitionSpec as P

MESH = pl.DeviceIdType.MESH
TOK = 256
HEADS = 8
HD = 128
NX = 4
NZ = 8
ROW = NX * TOK
OUT = 4096
MINE = 1024
HALF = MINE // 2
CHUNKS = 2
CR = TOK // CHUNKS
GROUPS = HEADS
PER = GROUPS // CHUNKS
LANES = 2 * CR
ONES = 16
LOG2E_SCALE = math.log2(math.e) / math.sqrt(HD)
NEG = -1e30
K, V = 0, 1
BOTH = ((K,), (V,))


def kernel(
    q_hbm, k_hbm, v_hbm, w_hbm, d_ref, out_ref,
    qst, vst, qt, kb, vt, kx, vx, tk, tv, ok, ov, d2, acc, top, sa, sb, att, wv,
    snd_a, rcv_a, snd_n, rcv_n,
    lsem, wsem, gs, gr, tr, osem, ds, dr,
):
    ctx = lax.axis_index("ctx")
    y = lax.axis_index("tp")
    z, x = ctx // NX, ctx % NX
    xp, xm, xo = (x + 1) % NX, (x + NX - 1) % NX, (x + 2) % NX
    dev_xp, dev_xm, dev_xo = z * NX + xp, z * NX + xm, z * NX + xo

    def plane(dz):
        return ((z + dz + NZ) % NZ) * NX + x

    dev_zp = plane(1)
    yp, ym, yo = (y + 1) % 4, (y + 3) % 4, (y + 2) % 4

    kcp = pltpu.make_async_copy(k_hbm, kb.at[0, x], lsem.at[0])
    vcp = pltpu.make_async_copy(v_hbm, vst, lsem.at[1])
    kcp.start()
    vcp.start()
    barrier = pltpu.get_barrier_semaphore()
    for dev in (dev_xp, dev_xm, dev_xo, plane(1), plane(-1), plane(2), plane(-2)):
        pl.semaphore_signal(barrier, inc=1, device_id={"ctx": dev}, device_id_type=MESH)
    for dev in (yp, ym):
        pl.semaphore_signal(barrier, inc=1, device_id={"tp": dev}, device_id_type=MESH)
    qcp = pltpu.make_async_copy(q_hbm, qst, lsem.at[2])
    qcp.start()
    wcp = []
    for i in range(4):
        cp = pltpu.make_async_copy(w_hbm.at[pl.ds(i * 256, 256)], wv.at[pl.ds(i * 256, 256)], wsem.at[i])
        cp.start()
        wcp.append(cp)
    for c in range(CHUNKS):
        half = d_ref[:, c * CR : (c + 1) * CR]
        d2[c] = jnp.concatenate([half, half], axis=1)
    acc[...] = jnp.zeros_like(acc)
    top[...] = jnp.full_like(top, NEG)
    vcp.wait()
    vt[0, x] = vst[...].T
    kcp.wait()
    qcp.wait()
    for c in range(CHUNKS):
        for h in range(HEADS):
            part = qst[c * CR : (c + 1) * CR, h * HD : (h + 1) * HD].T
            qt[c * PER + h // 2, :, (h % 2) * CR : (h % 2 + 1) * CR] = part
    pl.semaphore_wait(barrier, 9)

    pending = []

    def buf(row, col, what):
        if row == 4:
            return (kx, vx)[what]
        if row == 5:
            return (tk, tv)[what]
        if row == 6:
            return (ok, ov)[what]
        return (kb, vt)[what].at[row, col]

    def arrival(row, col, what):
        if row == 5:
            return tr.at[what]
        if row == 6:
            return osem.at[what]
        return gr.at[row, 0 if row == 4 else col, what]

    def send(src, dst, dev, whats=(K, V), when=None):
        for what in whats:
            cp = pltpu.make_async_remote_copy(
                src_ref=buf(*src, what),
                dst_ref=buf(*dst, what),
                send_sem=gs.at[len(pending)],
                recv_sem=arrival(*dst, what),
                device_id={"ctx": dev},
                device_id_type=MESH,
            )
            pending.append((cp, when))
            if when is None:
                cp.start()
            else:
                pl.when(when)(cp.start)

    def take(row, col, whats=(K, V), when=None):
        for what in whats:
            ref = buf(row, col, what)
            cp = pltpu.make_async_copy(ref, ref, arrival(row, col, what))
            if when is None:
                cp.wait()
            else:
                pl.when(when)(cp.wait)

    for w in BOTH:
        send((0, x), (1, x), dev_zp, w)
        send((0, x), (0, x), dev_xp, w, x < 3)
        send((0, x), (0, x), dev_xo, w, x < 2)
        send((0, x), (6, x), dev_xo, w, x >= 2)
        send((0, x), (5, x), plane(-2), w)
        send((0, x), (0, x), dev_xm, w, x == 0)

    def sides(row, w):
        send((row, x), (row, x), dev_xp, w)
        send((row, x), (row, x), dev_xm, w)

    key_row = lax.broadcasted_iota(jnp.int32, (TOK, LANES), 0)

    def sweep(blocks, lo, hi, causal=False):
        tiles = [blocks[i : i + 2] for i in range(0, len(blocks), 2)]

        def scores(g, dst, causal):
            first = d2[g // PER]
            high = None
            for j, tile in enumerate(tiles):
                s = jnp.dot(
                    jnp.concatenate([b[0][...] for b in tile], axis=0), qt[g],
                    preferred_element_type=jnp.float32,
                )
                pos = jnp.concatenate([key_row + b[2] for b in tile], axis=0)
                allowed = pos >= first
                if causal and j == 0:
                    lane = lax.broadcasted_iota(jnp.int32, (1, LANES), 1)
                    at = ctx * TOK + (g // PER) * CR + lane % CR
                    allowed = allowed & (pos <= at)
                s = jnp.where(allowed, s, NEG)
                dst[j, : s.shape[0]] = s
                part = jnp.max(s.reshape(s.shape[0] // 8, 8, LANES), axis=0)
                high = part if high is None else jnp.maximum(high, part)
            return high

        def absorb(g, src, high, nxt):
            old = top[g]
            new = jnp.maximum(old, jnp.max(high, axis=0, keepdims=True))
            top[g] = new
            factor = jnp.exp2((old - new) * LOG2E_SCALE)
            after = scores(jnp.minimum(g + 1, hi - 1), nxt, causal)
            total = None
            for j, tile in enumerate(tiles):
                n = len(tile) * TOK
                p = jnp.exp2((src[j, :n] - new) * LOG2E_SCALE).astype(jnp.bfloat16)
                values = jnp.concatenate([b[1][...] for b in tile], axis=1)
                values = jnp.concatenate([values, jnp.ones((ONES, n), jnp.bfloat16)], axis=0)
                part = jnp.dot(values, p, preferred_element_type=jnp.float32)
                total = part if total is None else total + part
            acc[g] = acc[g] * factor + total
            return after

        def two(t, high):
            g = lo + 2 * t
            high = absorb(g, sa, high, sb)
            return absorb(g + 1, sb, high, sa)

        lax.fori_loop(0, (hi - lo) // 2, two, scores(lo, sa, causal))

    def block(row, col, first):
        return (buf(row, col, K), buf(row, col, V), first)

    def far(row, col):
        return block(row, col, (z - row) * ROW + col * TOK)

    def mixed(col):
        return block(0, col, (z - jnp.where(col < x, 0, 4)) * ROW + col * TOK)

    for w in BOTH:
        take(1, x, w)
        send((1, x), (2, x), dev_zp, w)
        sides(1, w)
    for w in BOTH:
        take(5, x, w)
        send((5, x), (4, x), plane(-2), w)
    for w in BOTH:
        take(6, x, w, x < 2)
        send((6, x), (1, xo), dev_zp, w, x < 2)
        take(0, xo, w, x >= 2)
        send((0, xo), (1, xo), dev_zp, w, x >= 2)
    for w in BOTH:
        take(2, x, w)
        send((2, x), (3, x), dev_zp, w)
        sides(2, w)
    take(1, xp)
    take(1, xm)
    sweep([block(0, x, ctx * TOK), far(1, x), far(1, xp), far(1, xm)], 0, GROUPS, causal=True)
    for w in BOTH:
        take(1, xo, w)
        send((1, xo), (2, xo), dev_zp, w)
    for w in BOTH:
        take(4, x, w)
        send((4, x), (0, x), dev_xm, w, x > 0)
        send((4, x), (0, x), dev_xo, w, x > 1)
        send((4, x), (0, x), dev_xp, w, x == 3)
    for w in BOTH:
        take(3, x, w)
        sides(3, w)
    take(2, xp)
    take(2, xm)
    sweep([far(1, xo), far(2, x), far(2, xp), far(2, xm)], 0, GROUPS)
    for w in BOTH:
        take(2, xo, w)
        send((2, xo), (3, xo), dev_zp, w)
    take(0, xp)
    take(0, xm)
    sweep([far(2, xo), mixed(xp), mixed(xm), block(4, x, (z - 4) * ROW + x * TOK)], 0, GROUPS)
    take(3, xp)
    take(3, xm)
    take(0, xo, when=x < 2)
    for cp in wcp:
        cp.wait()

    def rs_copy(c, slot, src, dst, dev):
        return pltpu.make_async_remote_copy(
            src_ref=src,
            dst_ref=dst,
            send_sem=ds.at[c, slot],
            recv_sem=dr.at[c, slot],
            device_id={"tp": dev},
            device_id_type=MESH,
        )

    def copies(c):
        return (
            rs_copy(c, 0, snd_a.at[c, 0], rcv_a.at[c, 0], yp),
            rs_copy(c, 1, snd_a.at[c, 1], rcv_a.at[c, 1], ym),
            rs_copy(c, 2, snd_n.at[c, 0], rcv_n.at[c, 0], yp),
            rs_copy(c, 3, snd_n.at[c, 1], rcv_n.at[c, 1], ym),
            rs_copy(c, 4, snd_n.at[c, 2], rcv_n.at[c, 2], yp),
            rs_copy(c, 5, snd_n.at[c, 3], rcv_n.at[c, 3], ym),
        )

    def project(c, dest, half):
        cols = pl.ds(pl.multiple_of(dest * MINE + half * HALF, HALF), HALF)
        return jnp.dot(att[c], wv[:, cols], preferred_element_type=jnp.float32)

    def finish(c):
        sweep([far(3, x), far(3, xp), far(3, xm), mixed(xo)], c * PER, (c + 1) * PER)
        if c == 0:
            take(3, xo)
        sweep([far(3, xo)], c * PER, (c + 1) * PER)
        for i in range(PER):
            a = acc[c * PER + i]
            o = a[:HD] / a[HD : HD + 1]
            for side in range(2):
                h = 2 * i + side
                att[c, :, h * HD : (h + 1) * HD] = o[:, side * CR : (side + 1) * CR].T.astype(jnp.bfloat16)
        cps = copies(c)
        for i, (dest, half, buffer, slot) in enumerate(
            ((yo, 0, snd_a, 0), (yo, 1, snd_a, 1), (yp, 1, snd_n, 0), (ym, 0, snd_n, 1))
        ):
            buffer[c, slot] = project(c, dest, half).astype(jnp.bfloat16)
            cps[i].start()

    def relay(c):
        cps = copies(c)
        for i, (dest, half) in enumerate(((yp, 0), (ym, 1))):
            part = project(c, dest, half)
            cps[i].wait_recv()
            snd_n[c, 2 + i] = (part + rcv_a[c, i].astype(jnp.float32)).astype(jnp.bfloat16)
            cps[4 + i].start()

    def collect(c):
        cps = copies(c)
        own = [project(c, y, half) for half in (0, 1)]
        for i in range(2, 6):
            cps[i].wait_recv()
        rows = slice(c * CR, (c + 1) * CR)
        out_ref[rows, :HALF] = (
            own[0] + rcv_n[c, 2].astype(jnp.float32) + rcv_n[c, 1].astype(jnp.float32)
        ).astype(jnp.bfloat16)
        out_ref[rows, HALF:] = (
            own[1] + rcv_n[c, 0].astype(jnp.float32) + rcv_n[c, 3].astype(jnp.float32)
        ).astype(jnp.bfloat16)

    finish(0)
    finish(1)
    relay(0)
    relay(1)
    collect(0)
    collect(1)
    for c in range(CHUNKS):
        for cp in copies(c):
            cp.wait_send()
    for cp, when in pending:
        if when is None:
            cp.wait_send()
        else:
            pl.when(when)(cp.wait_send)


def body(queries, keys, values, out_weight, doc_ids):
    bf, f32 = jnp.bfloat16, jnp.float32
    hbm = pl.BlockSpec(memory_space=pltpu.HBM)
    vmem = pl.BlockSpec(memory_space=pltpu.VMEM)
    dma = pltpu.SemaphoreType.DMA
    return pl.pallas_call(
        kernel,
        out_shape=jax.ShapeDtypeStruct((TOK, MINE), bf),
        in_specs=[hbm] * 4 + [vmem],
        out_specs=vmem,
        scratch_shapes=[
            pltpu.VMEM((TOK, HEADS * HD), bf),
            pltpu.VMEM((TOK, HD), bf),
            pltpu.VMEM((GROUPS, HD, LANES), bf),
            pltpu.VMEM((4, NX, TOK, HD), bf),
            pltpu.VMEM((4, NX, HD, TOK), bf),
            pltpu.VMEM((TOK, HD), bf),
            pltpu.VMEM((HD, TOK), bf),
            pltpu.VMEM((TOK, HD), bf),
            pltpu.VMEM((HD, TOK), bf),
            pltpu.VMEM((TOK, HD), bf),
            pltpu.VMEM((HD, TOK), bf),
            pltpu.VMEM((CHUNKS, 1, LANES), jnp.int32),
            pltpu.VMEM((GROUPS, HD + ONES, LANES), f32),
            pltpu.VMEM((GROUPS, 1, LANES), f32),
            pltpu.VMEM((2, 2 * TOK, LANES), f32),
            pltpu.VMEM((2, 2 * TOK, LANES), f32),
            pltpu.VMEM((CHUNKS, CR, HEADS * HD), bf),
            pltpu.VMEM((HEADS * HD, OUT), bf),
            pltpu.VMEM((CHUNKS, 2, CR, HALF), bf),
            pltpu.VMEM((CHUNKS, 2, CR, HALF), bf),
            pltpu.VMEM((CHUNKS, 4, CR, HALF), bf),
            pltpu.VMEM((CHUNKS, 4, CR, HALF), bf),
            dma((3,)),
            dma((4,)),
            dma((64,)),
            dma((5, NX, 2)),
            dma((2,)),
            dma((2,)),
            dma((CHUNKS, 6)),
            dma((CHUNKS, 6)),
        ],
        compiler_params=pltpu.CompilerParams(
            collective_id=0, has_side_effects=True, vmem_limit_bytes=60 << 20
        ),
        cost_estimate=pl.CostEstimate(flops=7 * 10**9, bytes_accessed=10**7, transcendentals=9 * 10**6),
    )(queries, keys, values, out_weight, doc_ids.reshape(1, TOK))


def solution(mesh):
    placed = (
        P(("dp", "ctx"), "tp"),
        P(("dp", "ctx"), "tp"),
        P(("dp", "ctx"), "tp"),
        P("tp", None),
        P(("dp", "ctx")),
    )
    return jax.shard_map(
        body, mesh=mesh, in_specs=placed, out_specs=P(("dp", "ctx"), "tp"), check_vma=False
    )
```

```python
import math

import jax
import jax.numpy as jnp
from jax import lax
from jax.experimental import pallas as pl
from jax.experimental.pallas import tpu as pltpu
from jax.sharding import PartitionSpec as P

MESH = pl.DeviceIdType.MESH
TOK = 256
HEADS = 8
HD = 128
NX = 4
NZ = 8
ROW = NX * TOK
OUT = 4096
MINE = 1024
HALF = MINE // 2
CHUNKS = 4
CR = TOK // CHUNKS
LANES = 256
SIDE = LANES // CR
PER = HEADS // SIDE
GROUPS = CHUNKS * PER
ONES = 16
LOG2E_SCALE = math.log2(math.e) / math.sqrt(HD)
NEG = -1e30
K, V = 0, 1
BOTH = ((K,), (V,))


def kernel(
    q_hbm, k_hbm, v_hbm, w_hbm, d_ref, out_ref,
    qst, vst, qt, kb, vt, kx, vx, tk, tv, ok, ov, d2, acc, top, sa, sb, att, wv,
    snd_a, rcv_a, snd_n, rcv_n,
    lsem, wsem, gs, gr, tr, osem, ds, dr,
):
    ctx = lax.axis_index("ctx")
    y = lax.axis_index("tp")
    z, x = ctx // NX, ctx % NX
    xp, xm, xo = (x + 1) % NX, (x + NX - 1) % NX, (x + 2) % NX
    dev_xp, dev_xm, dev_xo = z * NX + xp, z * NX + xm, z * NX + xo

    def plane(dz):
        return ((z + dz + NZ) % NZ) * NX + x

    dev_zp = plane(1)
    yp, ym, yo = (y + 1) % 4, (y + 3) % 4, (y + 2) % 4

    kcp = pltpu.make_async_copy(k_hbm, kb.at[0, x], lsem.at[0])
    vcp = pltpu.make_async_copy(v_hbm, vst, lsem.at[1])
    kcp.start()
    vcp.start()
    barrier = pltpu.get_barrier_semaphore()
    for dev in (dev_xp, dev_xm, dev_xo, plane(1), plane(-1), plane(2), plane(-2)):
        pl.semaphore_signal(barrier, inc=1, device_id={"ctx": dev}, device_id_type=MESH)
    for dev in (yp, ym):
        pl.semaphore_signal(barrier, inc=1, device_id={"tp": dev}, device_id_type=MESH)
    qcp = pltpu.make_async_copy(q_hbm, qst, lsem.at[2])
    qcp.start()
    vcp.wait()
    vt[0, x] = vst[...].T
    kcp.wait()
    pl.semaphore_wait(barrier, 9)

    pending = []

    def buf(row, col, what):
        if row == 4:
            return (kx, vx)[what]
        if row == 5:
            return (tk, tv)[what]
        if row == 6:
            return (ok, ov)[what]
        return (kb, vt)[what].at[row, col]

    def arrival(row, col, what):
        if row == 5:
            return tr.at[what]
        if row == 6:
            return osem.at[what]
        return gr.at[row, 0 if row == 4 else col, what]

    def send(src, dst, dev, whats=(K, V), when=None):
        for what in whats:
            cp = pltpu.make_async_remote_copy(
                src_ref=buf(*src, what),
                dst_ref=buf(*dst, what),
                send_sem=gs.at[len(pending)],
                recv_sem=arrival(*dst, what),
                device_id={"ctx": dev},
                device_id_type=MESH,
            )
            pending.append((cp, when))
            if when is None:
                cp.start()
            else:
                pl.when(when)(cp.start)

    def take(row, col, whats=(K, V), when=None):
        for what in whats:
            ref = buf(row, col, what)
            cp = pltpu.make_async_copy(ref, ref, arrival(row, col, what))
            if when is None:
                cp.wait()
            else:
                pl.when(when)(cp.wait)

    for w in BOTH:
        send((0, x), (1, x), dev_zp, w)
        send((0, x), (0, x), dev_xp, w, x < 3)
        send((0, x), (0, x), dev_xo, w, x < 2)
        send((0, x), (6, x), dev_xo, w, x >= 2)
        send((0, x), (5, x), plane(-2), w)
        send((0, x), (0, x), dev_xm, w, x == 0)

    for c in range(CHUNKS):
        d2[c] = jnp.concatenate([d_ref[:, c * CR : (c + 1) * CR]] * SIDE, axis=1)
    acc[...] = jnp.zeros_like(acc)
    top[...] = jnp.full_like(top, NEG)
    qcp.wait()
    for c in range(CHUNKS):
        for i in range(PER):
            heads = range(i * SIDE, (i + 1) * SIDE)
            part = [qst[c * CR : (c + 1) * CR, h * HD : (h + 1) * HD] for h in heads]
            qt[c * PER + i] = jnp.concatenate(part, axis=0).T

    def sides(row, w):
        send((row, x), (row, x), dev_xp, w)
        send((row, x), (row, x), dev_xm, w)

    key_row = lax.broadcasted_iota(jnp.int32, (TOK, LANES), 0)

    def sweep(blocks, lo, count, causal=False):
        hi = lo + count
        tiles = [blocks[i : i + 2] for i in range(0, len(blocks), 2)]

        def scores(g, dst, causal):
            first = d2[g // PER]
            high = None
            for j, tile in enumerate(tiles):
                s = jnp.dot(
                    jnp.concatenate([b[0][...] for b in tile], axis=0), qt[g],
                    preferred_element_type=jnp.float32,
                )
                pos = jnp.concatenate([key_row + b[2] for b in tile], axis=0)
                allowed = pos >= first
                if causal and j == 0:
                    lane = lax.broadcasted_iota(jnp.int32, (1, LANES), 1)
                    at = ctx * TOK + (g // PER) * CR + lane % CR
                    allowed = allowed & (pos <= at)
                s = jnp.where(allowed, s, NEG)
                dst[j, : s.shape[0]] = s
                part = jnp.max(s.reshape(s.shape[0] // 8, 8, LANES), axis=0)
                high = part if high is None else jnp.maximum(high, part)
            return high

        def absorb(g, src, high, nxt, more=True):
            old = top[g]
            new = jnp.maximum(old, jnp.max(high, axis=0, keepdims=True))
            top[g] = new
            factor = jnp.exp2((old - new) * LOG2E_SCALE)
            after = scores(jnp.minimum(g + 1, hi - 1), nxt, causal) if more else None
            total = None
            for j, tile in enumerate(tiles):
                n = len(tile) * TOK
                p = jnp.exp2((src[j, :n] - new) * LOG2E_SCALE).astype(jnp.bfloat16)
                values = jnp.concatenate([b[1][...] for b in tile], axis=1)
                values = jnp.concatenate([values, jnp.ones((ONES, n), jnp.bfloat16)], axis=0)
                part = jnp.dot(values, p, preferred_element_type=jnp.float32)
                total = part if total is None else total + part
            acc[g] = acc[g] * factor + total
            return after

        high = scores(lo, sa, causal)
        if count == 2:
            absorb(lo + 1, sb, absorb(lo, sa, high, sb), sa, more=False)
            return

        def two(t, high):
            g = lo + 2 * t
            high = absorb(g, sa, high, sb)
            return absorb(g + 1, sb, high, sa)

        lax.fori_loop(0, count // 2, two, high)

    def block(row, col, first):
        return (buf(row, col, K), buf(row, col, V), first)

    def far(row, col):
        return block(row, col, (z - row) * ROW + col * TOK)

    def mixed(col):
        return block(0, col, (z - jnp.where(col < x, 0, 4)) * ROW + col * TOK)

    for w in BOTH:
        take(1, x, w)
        send((1, x), (2, x), dev_zp, w)
        sides(1, w)
    for w in BOTH:
        take(6, x, w, x < 2)
        send((6, x), (1, xo), dev_zp, w, x < 2)
        take(0, xo, w, x >= 2)
        send((0, xo), (1, xo), dev_zp, w, x >= 2)
    wcp = []
    for i in range(4):
        cp = pltpu.make_async_copy(w_hbm.at[pl.ds(i * 256, 256)], wv.at[pl.ds(i * 256, 256)], wsem.at[i])
        cp.start()
        wcp.append(cp)
    for w in BOTH:
        take(5, x, w)
        send((5, x), (4, x), plane(-2), w)
    for w in BOTH:
        take(2, x, w)
        send((2, x), (3, x), dev_zp, w)
        sides(2, w)
    take(1, xp)
    take(1, xm)
    near = [block(0, x, ctx * TOK), far(1, x), far(1, xp), far(1, xm)]
    sweep(near, 0, GROUPS // 2, causal=True)
    for w in BOTH:
        take(1, xo, w)
        send((1, xo), (2, xo), dev_zp, w)
    for w in BOTH:
        take(4, x, w)
        send((4, x), (0, x), dev_xo, w, x > 1)
        send((4, x), (0, x), dev_xm, w, x > 0)
        send((4, x), (0, x), dev_xp, w, x == 3)
    sweep(near, GROUPS // 2, GROUPS // 2, causal=True)
    for w in BOTH:
        take(3, x, w)
        sides(3, w)
    sweep([far(1, xo), far(2, x), far(3, x), block(4, x, (z - 4) * ROW + x * TOK)], 0, GROUPS)
    for w in BOTH:
        take(2, xo, w)
        send((2, xo), (3, xo), dev_zp, w)
    take(2, xp)
    take(2, xm)
    take(0, xp)
    take(0, xm)
    sweep([far(2, xp), far(2, xm), mixed(xp), mixed(xm)], 0, GROUPS)
    take(3, xp)
    take(3, xm)
    take(0, xo, when=x < 2)
    take(3, xo)
    for cp in wcp:
        cp.wait()

    def rs_copy(c, slot, src, dst, dev):
        return pltpu.make_async_remote_copy(
            src_ref=src,
            dst_ref=dst,
            send_sem=ds.at[c, slot],
            recv_sem=dr.at[c, slot],
            device_id={"tp": dev},
            device_id_type=MESH,
        )

    def copies(c):
        return (
            rs_copy(c, 0, snd_a.at[c, 0], rcv_a.at[c, 0], yp),
            rs_copy(c, 1, snd_a.at[c, 1], rcv_a.at[c, 1], ym),
            rs_copy(c, 2, snd_n.at[c, 0], rcv_n.at[c, 0], yp),
            rs_copy(c, 3, snd_n.at[c, 1], rcv_n.at[c, 1], ym),
            rs_copy(c, 4, snd_n.at[c, 2], rcv_n.at[c, 2], yp),
            rs_copy(c, 5, snd_n.at[c, 3], rcv_n.at[c, 3], ym),
        )

    def project(c, dest, half):
        cols = pl.ds(pl.multiple_of(dest * MINE + half * HALF, HALF), HALF)
        return jnp.dot(att[c], wv[:, cols], preferred_element_type=jnp.float32)

    def finish(c, carry):
        sweep([far(2, xo), far(3, xp), far(3, xm), mixed(xo), far(3, xo)], c * PER, PER)
        for i in range(PER):
            a = acc[c * PER + i]
            o = (a[:HD] / a[HD : HD + 1]).T.astype(jnp.bfloat16)
            for side in range(SIDE):
                h = i * SIDE + side
                att[c, :, h * HD : (h + 1) * HD] = o[side * CR : (side + 1) * CR]
        cps = copies(c)
        for i, (dest, half, buffer, slot) in enumerate(
            ((yo, 0, snd_a, 0), (yo, 1, snd_a, 1), (yp, 1, snd_n, 0), (ym, 0, snd_n, 1))
        ):
            buffer[c, slot] = project(c, dest, half).astype(jnp.bfloat16)
            cps[i].start()
        return carry

    def relay(c, carry):
        cps = copies(c)
        for i, (dest, half) in enumerate(((yp, 0), (ym, 1))):
            part = project(c, dest, half)
            cps[i].wait_recv()
            snd_n[c, 2 + i] = (part + rcv_a[c, i].astype(jnp.float32)).astype(jnp.bfloat16)
            cps[4 + i].start()
        return carry

    def collect(c, carry):
        cps = copies(c)
        own = [project(c, y, half) for half in (0, 1)]
        for i in range(2, 6):
            cps[i].wait_recv()
        rows = pl.ds(pl.multiple_of(c * CR, CR), CR)
        out_ref[rows, :HALF] = (
            own[0] + rcv_n[c, 2].astype(jnp.float32) + rcv_n[c, 1].astype(jnp.float32)
        ).astype(jnp.bfloat16)
        out_ref[rows, HALF:] = (
            own[1] + rcv_n[c, 0].astype(jnp.float32) + rcv_n[c, 3].astype(jnp.float32)
        ).astype(jnp.bfloat16)
        for cp in cps:
            cp.wait_send()
        return carry

    lax.fori_loop(0, CHUNKS, finish, 0)
    lax.fori_loop(0, CHUNKS, relay, 0)
    lax.fori_loop(0, CHUNKS, collect, 0)
    for cp, when in pending:
        if when is None:
            cp.wait_send()
        else:
            pl.when(when)(cp.wait_send)


def body(queries, keys, values, out_weight, doc_ids):
    bf, f32 = jnp.bfloat16, jnp.float32
    hbm = pl.BlockSpec(memory_space=pltpu.HBM)
    vmem = pl.BlockSpec(memory_space=pltpu.VMEM)
    dma = pltpu.SemaphoreType.DMA
    return pl.pallas_call(
        kernel,
        out_shape=jax.ShapeDtypeStruct((TOK, MINE), bf),
        in_specs=[hbm] * 4 + [vmem],
        out_specs=vmem,
        scratch_shapes=[
            pltpu.VMEM((TOK, HEADS * HD), bf),
            pltpu.VMEM((TOK, HD), bf),
            pltpu.VMEM((GROUPS, HD, LANES), bf),
            pltpu.VMEM((4, NX, TOK, HD), bf),
            pltpu.VMEM((4, NX, HD, TOK), bf),
            pltpu.VMEM((TOK, HD), bf),
            pltpu.VMEM((HD, TOK), bf),
            pltpu.VMEM((TOK, HD), bf),
            pltpu.VMEM((HD, TOK), bf),
            pltpu.VMEM((TOK, HD), bf),
            pltpu.VMEM((HD, TOK), bf),
            pltpu.VMEM((CHUNKS, 1, LANES), jnp.int32),
            pltpu.VMEM((GROUPS, HD + ONES, LANES), f32),
            pltpu.VMEM((GROUPS, 1, LANES), f32),
            pltpu.VMEM((3, 2 * TOK, LANES), f32),
            pltpu.VMEM((3, 2 * TOK, LANES), f32),
            pltpu.VMEM((CHUNKS, CR, HEADS * HD), bf),
            pltpu.VMEM((HEADS * HD, OUT), bf),
            pltpu.VMEM((CHUNKS, 2, CR, HALF), bf),
            pltpu.VMEM((CHUNKS, 2, CR, HALF), bf),
            pltpu.VMEM((CHUNKS, 4, CR, HALF), bf),
            pltpu.VMEM((CHUNKS, 4, CR, HALF), bf),
            dma((3,)),
            dma((4,)),
            dma((64,)),
            dma((5, NX, 2)),
            dma((2,)),
            dma((2,)),
            dma((CHUNKS, 6)),
            dma((CHUNKS, 6)),
        ],
        compiler_params=pltpu.CompilerParams(
            collective_id=0, has_side_effects=True, vmem_limit_bytes=60 << 20
        ),
        cost_estimate=pl.CostEstimate(flops=7 * 10**9, bytes_accessed=10**7, transcendentals=9 * 10**6),
    )(queries, keys, values, out_weight, doc_ids.reshape(1, TOK))


def solution(mesh):
    placed = (
        P(("dp", "ctx"), "tp"),
        P(("dp", "ctx"), "tp"),
        P(("dp", "ctx"), "tp"),
        P("tp", None),
        P(("dp", "ctx")),
    )
    return jax.shard_map(
        body, mesh=mesh, in_specs=placed, out_specs=P(("dp", "ctx"), "tp"), check_vma=False
    )
```

```python
import math

import jax
import jax.numpy as jnp
from jax import lax
from jax.experimental import pallas as pl
from jax.experimental.pallas import tpu as pltpu
from jax.sharding import PartitionSpec as P

MESH = pl.DeviceIdType.MESH
TOK = 256
HEADS = 8
HD = 128
NX = 4
NZ = 8
ROW = NX * TOK
OUT = 4096
MINE = 1024
HALF = MINE // 2
CHUNKS = 4
CR = TOK // CHUNKS
LANES = 256
SIDE = LANES // CR
PER = HEADS // SIDE
GROUPS = CHUNKS * PER
ONES = 16
LOG2E_SCALE = math.log2(math.e) / math.sqrt(HD)
NEG = -1e30
K, V = 0, 1
BOTH = ((K,), (V,))


def kernel(
    q_hbm, k_hbm, v_hbm, w_hbm, d_ref, out_hbm,
    qst, vst, qt, kb, vt, kx, vx, tk, tv, ok, ov, d2, acc, top, sa, sb, att, wv, out,
    snd_a, rcv_a, snd_n, rcv_n,
    lsem, wsem, gs, gr, tr, osem, ds, dr, osems,
):
    ctx = lax.axis_index("ctx")
    y = lax.axis_index("tp")
    z, x = ctx // NX, ctx % NX
    xp, xm, xo = (x + 1) % NX, (x + NX - 1) % NX, (x + 2) % NX
    dev_xp, dev_xm, dev_xo = z * NX + xp, z * NX + xm, z * NX + xo

    def plane(dz):
        return ((z + dz + NZ) % NZ) * NX + x

    dev_zp = plane(1)
    yp, ym, yo = (y + 1) % 4, (y + 3) % 4, (y + 2) % 4

    kcp = pltpu.make_async_copy(k_hbm, kb.at[0, x], lsem.at[0])
    vcp = pltpu.make_async_copy(v_hbm, vst, lsem.at[1])
    kcp.start()
    vcp.start()
    barrier = pltpu.get_barrier_semaphore()
    for dev in (dev_xp, dev_xm, dev_xo, plane(1), plane(-1), plane(2), plane(-2)):
        pl.semaphore_signal(barrier, inc=1, device_id={"ctx": dev}, device_id_type=MESH)
    for dev in (yp, ym):
        pl.semaphore_signal(barrier, inc=1, device_id={"tp": dev}, device_id_type=MESH)
    qcp = pltpu.make_async_copy(q_hbm, qst, lsem.at[2])
    qcp.start()
    vcp.wait()
    vt[0, x] = vst[...].T
    kcp.wait()
    pl.semaphore_wait(barrier, 9)

    pending = []

    def buf(row, col, what):
        if row == 4:
            return (kx, vx)[what]
        if row == 5:
            return (tk, tv)[what]
        if row == 6:
            return (ok, ov)[what]
        return (kb, vt)[what].at[row, col]

    def arrival(row, col, what):
        if row == 5:
            return tr.at[what]
        if row == 6:
            return osem.at[what]
        return gr.at[row, 0 if row == 4 else col, what]

    def send(src, dst, dev, whats=(K, V), when=None):
        for what in whats:
            cp = pltpu.make_async_remote_copy(
                src_ref=buf(*src, what),
                dst_ref=buf(*dst, what),
                send_sem=gs.at[len(pending)],
                recv_sem=arrival(*dst, what),
                device_id={"ctx": dev},
                device_id_type=MESH,
            )
            pending.append((cp, when))
            if when is None:
                cp.start()
            else:
                pl.when(when)(cp.start)

    def take(row, col, whats=(K, V), when=None):
        for what in whats:
            ref = buf(row, col, what)
            cp = pltpu.make_async_copy(ref, ref, arrival(row, col, what))
            if when is None:
                cp.wait()
            else:
                pl.when(when)(cp.wait)

    for w in BOTH:
        send((0, x), (1, x), dev_zp, w)
        send((0, x), (0, x), dev_xp, w, x < 3)
        send((0, x), (0, x), dev_xo, w, x < 2)
        send((0, x), (6, x), dev_xo, w, x >= 2)
        send((0, x), (5, x), plane(-2), w)
        send((0, x), (0, x), dev_xm, w, x == 0)

    for c in range(CHUNKS):
        d2[c] = jnp.concatenate([d_ref[:, c * CR : (c + 1) * CR]] * SIDE, axis=1)
    acc[...] = jnp.zeros_like(acc)
    top[...] = jnp.full_like(top, NEG)
    qcp.wait()
    for c in range(CHUNKS):
        for i in range(PER):
            heads = range(i * SIDE, (i + 1) * SIDE)
            part = [qst[c * CR : (c + 1) * CR, h * HD : (h + 1) * HD] for h in heads]
            qt[c * PER + i] = jnp.concatenate(part, axis=0).T

    def sides(row, w):
        send((row, x), (row, x), dev_xp, w)
        send((row, x), (row, x), dev_xm, w)

    key_row = lax.broadcasted_iota(jnp.int32, (TOK, LANES), 0)

    def sweep(blocks, lo, count, causal=False):
        hi = lo + count
        tiles = [blocks[i : i + 2] for i in range(0, len(blocks), 2)]

        def scores(g, dst, causal):
            first = d2[g // PER]
            high = None
            for j, tile in enumerate(tiles):
                s = jnp.dot(
                    jnp.concatenate([b[0][...] for b in tile], axis=0), qt[g],
                    preferred_element_type=jnp.float32,
                )
                pos = jnp.concatenate([key_row + b[2] for b in tile], axis=0)
                allowed = pos >= first
                if causal and j == 0:
                    lane = lax.broadcasted_iota(jnp.int32, (1, LANES), 1)
                    at = ctx * TOK + (g // PER) * CR + lane % CR
                    allowed = allowed & (pos <= at)
                s = jnp.where(allowed, s, NEG)
                dst[j, : s.shape[0]] = s
                part = jnp.max(s.reshape(s.shape[0] // 8, 8, LANES), axis=0)
                high = part if high is None else jnp.maximum(high, part)
            return high

        def absorb(g, src, high, nxt, more=True):
            old = top[g]
            new = jnp.maximum(old, jnp.max(high, axis=0, keepdims=True))
            top[g] = new
            factor = jnp.exp2((old - new) * LOG2E_SCALE)
            after = scores(g + 1, nxt, causal) if more else None
            total = None
            for j, tile in enumerate(tiles):
                n = len(tile) * TOK
                p = jnp.exp2((src[j, :n] - new) * LOG2E_SCALE).astype(jnp.bfloat16)
                values = jnp.concatenate([b[1][...] for b in tile], axis=1)
                values = jnp.concatenate([values, jnp.ones((ONES, n), jnp.bfloat16)], axis=0)
                part = jnp.dot(values, p, preferred_element_type=jnp.float32)
                total = part if total is None else total + part
            acc[g] = acc[g] * factor + total
            return after

        def two(t, high):
            g = lo + 2 * t
            high = absorb(g, sa, high, sb)
            return absorb(g + 1, sb, high, sa)

        high = scores(lo, sa, causal)
        if count > 2:
            high = lax.fori_loop(0, count // 2 - 1, two, high)
        absorb(hi - 1, sb, absorb(hi - 2, sa, high, sb), sa, more=False)

    def block(row, col, first):
        return (buf(row, col, K), buf(row, col, V), first)

    def far(row, col):
        return block(row, col, (z - row) * ROW + col * TOK)

    def mixed(col):
        return block(0, col, (z - jnp.where(col < x, 0, 4)) * ROW + col * TOK)

    for w in BOTH:
        take(1, x, w)
        send((1, x), (2, x), dev_zp, w)
        sides(1, w)
    for w in BOTH:
        take(5, x, w)
        send((5, x), (4, x), plane(-2), w)
    for w in BOTH:
        take(6, x, w, x < 2)
        send((6, x), (1, xo), dev_zp, w, x < 2)
        take(0, xo, w, x >= 2)
        send((0, xo), (1, xo), dev_zp, w, x >= 2)
    wcp = []
    for i in range(4):
        cp = pltpu.make_async_copy(w_hbm.at[pl.ds(i * 256, 256)], wv.at[pl.ds(i * 256, 256)], wsem.at[i])
        cp.start()
        wcp.append(cp)
    for w in BOTH:
        take(2, x, w)
        send((2, x), (3, x), dev_zp, w)
        sides(2, w)
    take(1, xp)
    take(1, xm)
    near = [block(0, x, ctx * TOK), far(1, x), far(1, xp), far(1, xm)]
    sweep(near, 0, GROUPS // 2, causal=True)
    for w in BOTH:
        take(1, xo, w)
        send((1, xo), (2, xo), dev_zp, w)
    for w in BOTH:
        take(4, x, w)
        send((4, x), (0, x), dev_xo, w, x > 1)
        send((4, x), (0, x), dev_xm, w, x > 0)
        send((4, x), (0, x), dev_xp, w, x == 3)
    sweep(near, GROUPS // 2, GROUPS // 2, causal=True)
    for w in BOTH:
        take(3, x, w)
        sides(3, w)
    sweep([far(1, xo), far(2, x), far(3, x), block(4, x, (z - 4) * ROW + x * TOK)], 0, GROUPS)
    for w in BOTH:
        take(2, xo, w)
        send((2, xo), (3, xo), dev_zp, w)
    take(2, xp)
    take(2, xm)
    take(0, xp)
    take(0, xm)
    sweep([far(2, xp), far(2, xm), mixed(xp), mixed(xm)], 0, GROUPS)
    take(3, xp)
    take(3, xm)
    take(0, xo, when=x < 2)
    take(3, xo)
    for cp in wcp:
        cp.wait()

    def rs_copy(c, slot, src, dst, dev):
        return pltpu.make_async_remote_copy(
            src_ref=src,
            dst_ref=dst,
            send_sem=ds.at[c, slot],
            recv_sem=dr.at[c, slot],
            device_id={"tp": dev},
            device_id_type=MESH,
        )

    def copies(c):
        return (
            rs_copy(c, 0, snd_a.at[c, 0], rcv_a.at[c, 0], yp),
            rs_copy(c, 1, snd_a.at[c, 1], rcv_a.at[c, 1], ym),
            rs_copy(c, 2, snd_n.at[c, 0], rcv_n.at[c, 0], yp),
            rs_copy(c, 3, snd_n.at[c, 1], rcv_n.at[c, 1], ym),
            rs_copy(c, 4, snd_n.at[c, 2], rcv_n.at[c, 2], yp),
            rs_copy(c, 5, snd_n.at[c, 3], rcv_n.at[c, 3], ym),
        )

    def project(c, dest, half):
        cols = pl.ds(pl.multiple_of(dest * MINE + half * HALF, HALF), HALF)
        return jnp.dot(att[c], wv[:, cols], preferred_element_type=jnp.float32)

    def finish(c, carry):
        sweep([far(2, xo), far(3, xp), far(3, xm), mixed(xo), far(3, xo)], c * PER, PER)
        for i in range(PER):
            a = acc[c * PER + i]
            o = (a[:HD] / a[HD : HD + 1]).T.astype(jnp.bfloat16)
            for side in range(SIDE):
                h = i * SIDE + side
                att[c, :, h * HD : (h + 1) * HD] = o[side * CR : (side + 1) * CR]
        cps = copies(c)
        for i, (dest, half, buffer, slot) in enumerate(
            ((yo, 0, snd_a, 0), (yo, 1, snd_a, 1), (yp, 1, snd_n, 0), (ym, 0, snd_n, 1))
        ):
            buffer[c, slot] = project(c, dest, half).astype(jnp.bfloat16)
            cps[i].start()
        return carry

    def relay(c, carry):
        cps = copies(c)
        for i, (dest, half) in enumerate(((yp, 0), (ym, 1))):
            part = project(c, dest, half)
            cps[i].wait_recv()
            snd_n[c, 2 + i] = (part + rcv_a[c, i].astype(jnp.float32)).astype(jnp.bfloat16)
            cps[4 + i].start()
        return carry

    def out_copy(c):
        rows = pl.ds(pl.multiple_of(c * CR, CR), CR)
        return pltpu.make_async_copy(out.at[rows], out_hbm.at[rows], osems.at[c])

    def collect(c, carry):
        cps = copies(c)
        own = [project(c, y, half) for half in (0, 1)]
        for i in range(2, 6):
            cps[i].wait_recv()
        rows = pl.ds(pl.multiple_of(c * CR, CR), CR)
        out[rows, :HALF] = (
            own[0] + rcv_n[c, 2].astype(jnp.float32) + rcv_n[c, 1].astype(jnp.float32)
        ).astype(jnp.bfloat16)
        out[rows, HALF:] = (
            own[1] + rcv_n[c, 0].astype(jnp.float32) + rcv_n[c, 3].astype(jnp.float32)
        ).astype(jnp.bfloat16)
        for cp in cps:
            cp.wait_send()
        out_copy(c).start()
        return carry

    lax.fori_loop(0, CHUNKS, finish, 0)
    lax.fori_loop(0, CHUNKS, relay, 0)
    lax.fori_loop(0, CHUNKS, collect, 0)
    for c in range(CHUNKS):
        out_copy(c).wait()
    for cp, when in pending:
        if when is None:
            cp.wait_send()
        else:
            pl.when(when)(cp.wait_send)


def body(queries, keys, values, out_weight, doc_ids):
    bf, f32 = jnp.bfloat16, jnp.float32
    hbm = pl.BlockSpec(memory_space=pltpu.HBM)
    vmem = pl.BlockSpec(memory_space=pltpu.VMEM)
    dma = pltpu.SemaphoreType.DMA
    return pl.pallas_call(
        kernel,
        out_shape=jax.ShapeDtypeStruct((TOK, MINE), bf),
        in_specs=[hbm] * 4 + [vmem],
        out_specs=hbm,
        scratch_shapes=[
            pltpu.VMEM((TOK, HEADS * HD), bf),
            pltpu.VMEM((TOK, HD), bf),
            pltpu.VMEM((GROUPS, HD, LANES), bf),
            pltpu.VMEM((4, NX, TOK, HD), bf),
            pltpu.VMEM((4, NX, HD, TOK), bf),
            pltpu.VMEM((TOK, HD), bf),
            pltpu.VMEM((HD, TOK), bf),
            pltpu.VMEM((TOK, HD), bf),
            pltpu.VMEM((HD, TOK), bf),
            pltpu.VMEM((TOK, HD), bf),
            pltpu.VMEM((HD, TOK), bf),
            pltpu.VMEM((CHUNKS, 1, LANES), jnp.int32),
            pltpu.VMEM((GROUPS, HD + ONES, LANES), f32),
            pltpu.VMEM((GROUPS, 1, LANES), f32),
            pltpu.VMEM((3, 2 * TOK, LANES), f32),
            pltpu.VMEM((3, 2 * TOK, LANES), f32),
            pltpu.VMEM((CHUNKS, CR, HEADS * HD), bf),
            pltpu.VMEM((HEADS * HD, OUT), bf),
            pltpu.VMEM((TOK, MINE), bf),
            pltpu.VMEM((CHUNKS, 2, CR, HALF), bf),
            pltpu.VMEM((CHUNKS, 2, CR, HALF), bf),
            pltpu.VMEM((CHUNKS, 4, CR, HALF), bf),
            pltpu.VMEM((CHUNKS, 4, CR, HALF), bf),
            dma((3,)),
            dma((4,)),
            dma((64,)),
            dma((5, NX, 2)),
            dma((2,)),
            dma((2,)),
            dma((CHUNKS, 6)),
            dma((CHUNKS, 6)),
            dma((CHUNKS,)),
        ],
        compiler_params=pltpu.CompilerParams(
            collective_id=0, has_side_effects=True, vmem_limit_bytes=60 << 20
        ),
        cost_estimate=pl.CostEstimate(flops=7 * 10**9, bytes_accessed=10**7, transcendentals=9 * 10**6),
    )(queries, keys, values, out_weight, doc_ids.reshape(1, TOK))


def solution(mesh):
    placed = (
        P(("dp", "ctx"), "tp"),
        P(("dp", "ctx"), "tp"),
        P(("dp", "ctx"), "tp"),
        P("tp", None),
        P(("dp", "ctx")),
    )
    return jax.shard_map(
        body, mesh=mesh, in_specs=placed, out_specs=P(("dp", "ctx"), "tp"), check_vma=False
    )
```

```python
import math

import jax
import jax.numpy as jnp
from jax import lax
from jax.experimental import pallas as pl
from jax.experimental.pallas import tpu as pltpu
from jax.sharding import PartitionSpec as P

MESH = pl.DeviceIdType.MESH
TOK = 256
HEADS = 8
HD = 128
NX = 4
NZ = 8
ROW = NX * TOK
OUT = 4096
MINE = 1024
HALF = MINE // 2
CHUNKS = 4
CR = TOK // CHUNKS
LANES = 256
SIDE = LANES // CR
PER = HEADS // SIDE
GROUPS = CHUNKS * PER
ONES = 16
LOG2E_SCALE = math.log2(math.e) / math.sqrt(HD)
NEG = -1e30
K, V = 0, 1
BOTH = ((K,), (V,))


def kernel(
    q_hbm, k_hbm, v_hbm, w_hbm, d_ref, out_hbm,
    qst, vst, qt, kb, vt, kx, vx, tk, tv, ok, ov, d2, acc, top, sa, sb, att, wv, out,
    snd_a, rcv_a, snd_n, rcv_n,
    lsem, wsem, gs, gr, tr, osem, ds, dr, osems,
):
    ctx = lax.axis_index("ctx")
    y = lax.axis_index("tp")
    z, x = ctx // NX, ctx % NX
    xp, xm, xo = (x + 1) % NX, (x + NX - 1) % NX, (x + 2) % NX
    dev_xp, dev_xm, dev_xo = z * NX + xp, z * NX + xm, z * NX + xo

    def plane(dz):
        return ((z + dz + NZ) % NZ) * NX + x

    dev_zp = plane(1)
    yp, ym, yo = (y + 1) % 4, (y + 3) % 4, (y + 2) % 4

    kcp = pltpu.make_async_copy(k_hbm, kb.at[0, x], lsem.at[0])
    vcp = pltpu.make_async_copy(v_hbm, vst, lsem.at[1])
    kcp.start()
    vcp.start()
    barrier = pltpu.get_barrier_semaphore()
    for dev in (dev_xp, dev_xm, dev_xo, plane(1), plane(-1), plane(2), plane(-2)):
        pl.semaphore_signal(barrier, inc=1, device_id={"ctx": dev}, device_id_type=MESH)
    for dev in (yp, ym):
        pl.semaphore_signal(barrier, inc=1, device_id={"tp": dev}, device_id_type=MESH)
    qcp = pltpu.make_async_copy(q_hbm, qst, lsem.at[2])
    qcp.start()
    vcp.wait()
    vt[0, x] = vst[...].T
    kcp.wait()
    pl.semaphore_wait(barrier, 9)

    pending = []

    def buf(row, col, what):
        if row == 4:
            return (kx, vx)[what]
        if row == 5:
            return (tk, tv)[what]
        if row == 6:
            return (ok, ov)[what]
        return (kb, vt)[what].at[row, col]

    def arrival(row, col, what):
        if row == 5:
            return tr.at[what]
        if row == 6:
            return osem.at[what]
        return gr.at[row, 0 if row == 4 else col, what]

    def send(src, dst, dev, whats=(K, V), when=None):
        for what in whats:
            cp = pltpu.make_async_remote_copy(
                src_ref=buf(*src, what),
                dst_ref=buf(*dst, what),
                send_sem=gs.at[len(pending)],
                recv_sem=arrival(*dst, what),
                device_id={"ctx": dev},
                device_id_type=MESH,
            )
            pending.append((cp, when))
            if when is None:
                cp.start()
            else:
                pl.when(when)(cp.start)

    def take(row, col, whats=(K, V), when=None):
        for what in whats:
            ref = buf(row, col, what)
            cp = pltpu.make_async_copy(ref, ref, arrival(row, col, what))
            if when is None:
                cp.wait()
            else:
                pl.when(when)(cp.wait)

    for w in BOTH:
        send((0, x), (1, x), dev_zp, w)
        send((0, x), (0, x), dev_xp, w, x < 3)
        send((0, x), (0, x), dev_xo, w, x < 2)
        send((0, x), (6, x), dev_xo, w, x >= 2)
        send((0, x), (5, x), plane(-2), w)
        send((0, x), (0, x), dev_xm, w, x == 0)

    for c in range(CHUNKS):
        d2[c] = jnp.concatenate([d_ref[:, c * CR : (c + 1) * CR]] * SIDE, axis=1)
    acc[...] = jnp.zeros_like(acc)
    top[...] = jnp.full_like(top, NEG)
    qcp.wait()
    for c in range(CHUNKS):
        for i in range(PER):
            heads = range(i * SIDE, (i + 1) * SIDE)
            part = [qst[c * CR : (c + 1) * CR, h * HD : (h + 1) * HD] for h in heads]
            qt[c * PER + i] = jnp.concatenate(part, axis=0).T

    def sides(row, w):
        send((row, x), (row, x), dev_xp, w)
        send((row, x), (row, x), dev_xm, w)

    key_row = lax.broadcasted_iota(jnp.int32, (TOK, LANES), 0)

    def sweep(blocks, lo, count, causal=False):
        hi = lo + count
        tiles = [blocks[i : i + 2] for i in range(0, len(blocks), 2)]

        def scores(g, dst, causal):
            first = d2[g // PER]
            high = None
            for j, tile in enumerate(tiles):
                s = jnp.dot(
                    jnp.concatenate([b[0][...] for b in tile], axis=0), qt[g],
                    preferred_element_type=jnp.float32,
                )
                pos = jnp.concatenate([key_row + b[2] for b in tile], axis=0)
                allowed = pos >= first
                if causal and j == 0:
                    lane = lax.broadcasted_iota(jnp.int32, (1, LANES), 1)
                    at = ctx * TOK + (g // PER) * CR + lane % CR
                    allowed = allowed & (pos <= at)
                s = jnp.where(allowed, s, NEG)
                dst[j, : s.shape[0]] = s
                part = jnp.max(s.reshape(s.shape[0] // 8, 8, LANES), axis=0)
                high = part if high is None else jnp.maximum(high, part)
            return high

        def absorb(g, src, high, nxt, more=True):
            old = top[g]
            new = jnp.maximum(old, jnp.max(high, axis=0, keepdims=True))
            top[g] = new
            factor = jnp.exp2((old - new) * LOG2E_SCALE)
            after = scores(g + 1, nxt, causal) if more else None
            total = None
            for j, tile in enumerate(tiles):
                n = len(tile) * TOK
                p = jnp.exp2((src[j, :n] - new) * LOG2E_SCALE).astype(jnp.bfloat16)
                values = jnp.concatenate([b[1][...] for b in tile], axis=1)
                values = jnp.concatenate([values, jnp.ones((ONES, n), jnp.bfloat16)], axis=0)
                part = jnp.dot(values, p, preferred_element_type=jnp.float32)
                total = part if total is None else total + part
            acc[g] = acc[g] * factor + total
            return after

        def two(t, high):
            g = lo + 2 * t
            high = absorb(g, sa, high, sb)
            return absorb(g + 1, sb, high, sa)

        high = scores(lo, sa, causal)
        if count > 2:
            high = lax.fori_loop(0, count // 2 - 1, two, high)
        absorb(hi - 1, sb, absorb(hi - 2, sa, high, sb), sa, more=False)

    def block(row, col, first):
        return (buf(row, col, K), buf(row, col, V), first)

    def far(row, col):
        return block(row, col, (z - row) * ROW + col * TOK)

    def mixed(col):
        return block(0, col, (z - jnp.where(col < x, 0, 4)) * ROW + col * TOK)

    for w in BOTH:
        take(1, x, w)
        send((1, x), (2, x), dev_zp, w)
        sides(1, w)
    for w in BOTH:
        take(5, x, w)
        send((5, x), (4, x), plane(-2), w)
    for w in BOTH:
        take(6, x, w, x < 2)
        send((6, x), (1, xo), dev_zp, w, x < 2)
        take(0, xo, w, x >= 2)
        send((0, xo), (1, xo), dev_zp, w, x >= 2)
    wcp = []
    for i in range(4):
        cp = pltpu.make_async_copy(w_hbm.at[pl.ds(i * 256, 256)], wv.at[pl.ds(i * 256, 256)], wsem.at[i])
        cp.start()
        wcp.append(cp)
    for w in BOTH:
        take(2, x, w)
        send((2, x), (3, x), dev_zp, w)
        sides(2, w)
    take(1, xp)
    take(1, xm)
    near = [block(0, x, ctx * TOK), far(1, x), far(1, xp), far(1, xm)]
    sweep(near, 0, GROUPS // 2, causal=True)
    for w in BOTH:
        take(1, xo, w)
        send((1, xo), (2, xo), dev_zp, w)
    for w in BOTH:
        take(4, x, w)
        send((4, x), (0, x), dev_xo, w, x > 1)
        send((4, x), (0, x), dev_xm, w, x > 0)
        send((4, x), (0, x), dev_xp, w, x == 3)
    sweep(near, GROUPS // 2, GROUPS // 2, causal=True)
    for w in BOTH:
        take(3, x, w)
        sides(3, w)
    older = [far(1, xo), far(2, x), far(3, x), block(4, x, (z - 4) * ROW + x * TOK)]
    sweep(older, 0, GROUPS // 2)
    for w in BOTH:
        take(2, xo, w)
        send((2, xo), (3, xo), dev_zp, w)
    sweep(older, GROUPS // 2, GROUPS // 2)
    take(2, xp)
    take(2, xm)
    take(0, xp)
    take(0, xm)
    sweep([far(2, xp), far(2, xm), mixed(xp), mixed(xm)], 0, GROUPS)
    take(3, xp)
    take(3, xm)
    take(0, xo, when=x < 2)
    take(3, xo)
    for cp in wcp:
        cp.wait()

    def rs_copy(c, slot, src, dst, dev):
        return pltpu.make_async_remote_copy(
            src_ref=src,
            dst_ref=dst,
            send_sem=ds.at[c, slot],
            recv_sem=dr.at[c, slot],
            device_id={"tp": dev},
            device_id_type=MESH,
        )

    def copies(c):
        return (
            rs_copy(c, 0, snd_a.at[c, 0], rcv_a.at[c, 0], yp),
            rs_copy(c, 1, snd_a.at[c, 1], rcv_a.at[c, 1], ym),
            rs_copy(c, 2, snd_n.at[c, 0], rcv_n.at[c, 0], yp),
            rs_copy(c, 3, snd_n.at[c, 1], rcv_n.at[c, 1], ym),
            rs_copy(c, 4, snd_n.at[c, 2], rcv_n.at[c, 2], yp),
            rs_copy(c, 5, snd_n.at[c, 3], rcv_n.at[c, 3], ym),
        )

    def project(c, dest, half):
        cols = pl.ds(pl.multiple_of(dest * MINE + half * HALF, HALF), HALF)
        return jnp.dot(att[c], wv[:, cols], preferred_element_type=jnp.float32)

    def finish(c, carry):
        sweep([far(2, xo), far(3, xp), far(3, xm), mixed(xo), far(3, xo)], c * PER, PER)
        for i in range(PER):
            a = acc[c * PER + i]
            o = (a[:HD] / a[HD : HD + 1]).T.astype(jnp.bfloat16)
            for side in range(SIDE):
                h = i * SIDE + side
                att[c, :, h * HD : (h + 1) * HD] = o[side * CR : (side + 1) * CR]
        cps = copies(c)
        for i, (dest, half, buffer, slot) in enumerate(
            ((yo, 0, snd_a, 0), (yo, 1, snd_a, 1), (yp, 1, snd_n, 0), (ym, 0, snd_n, 1))
        ):
            buffer[c, slot] = project(c, dest, half).astype(jnp.bfloat16)
            cps[i].start()
        return carry

    def relay(c, carry):
        cps = copies(c)
        for i, (dest, half) in enumerate(((yp, 0), (ym, 1))):
            part = project(c, dest, half)
            cps[i].wait_recv()
            snd_n[c, 2 + i] = (part + rcv_a[c, i].astype(jnp.float32)).astype(jnp.bfloat16)
            cps[4 + i].start()
        return carry

    def out_copy(c):
        rows = pl.ds(pl.multiple_of(c * CR, CR), CR)
        return pltpu.make_async_copy(out.at[rows], out_hbm.at[rows], osems.at[c])

    def collect(c, carry):
        cps = copies(c)
        own = [project(c, y, half) for half in (0, 1)]
        for i in range(2, 6):
            cps[i].wait_recv()
        rows = pl.ds(pl.multiple_of(c * CR, CR), CR)
        out[rows, :HALF] = (
            own[0] + rcv_n[c, 2].astype(jnp.float32) + rcv_n[c, 1].astype(jnp.float32)
        ).astype(jnp.bfloat16)
        out[rows, HALF:] = (
            own[1] + rcv_n[c, 0].astype(jnp.float32) + rcv_n[c, 3].astype(jnp.float32)
        ).astype(jnp.bfloat16)
        for cp in cps:
            cp.wait_send()
        out_copy(c).start()
        return carry

    lax.fori_loop(0, CHUNKS, finish, 0)
    lax.fori_loop(0, CHUNKS, relay, 0)
    lax.fori_loop(0, CHUNKS, collect, 0)
    for c in range(CHUNKS):
        out_copy(c).wait()
    for cp, when in pending:
        if when is None:
            cp.wait_send()
        else:
            pl.when(when)(cp.wait_send)


def body(queries, keys, values, out_weight, doc_ids):
    bf, f32 = jnp.bfloat16, jnp.float32
    hbm = pl.BlockSpec(memory_space=pltpu.HBM)
    vmem = pl.BlockSpec(memory_space=pltpu.VMEM)
    dma = pltpu.SemaphoreType.DMA
    return pl.pallas_call(
        kernel,
        out_shape=jax.ShapeDtypeStruct((TOK, MINE), bf),
        in_specs=[hbm] * 4 + [vmem],
        out_specs=hbm,
        scratch_shapes=[
            pltpu.VMEM((TOK, HEADS * HD), bf),
            pltpu.VMEM((TOK, HD), bf),
            pltpu.VMEM((GROUPS, HD, LANES), bf),
            pltpu.VMEM((4, NX, TOK, HD), bf),
            pltpu.VMEM((4, NX, HD, TOK), bf),
            pltpu.VMEM((TOK, HD), bf),
            pltpu.VMEM((HD, TOK), bf),
            pltpu.VMEM((TOK, HD), bf),
            pltpu.VMEM((HD, TOK), bf),
            pltpu.VMEM((TOK, HD), bf),
            pltpu.VMEM((HD, TOK), bf),
            pltpu.VMEM((CHUNKS, 1, LANES), jnp.int32),
            pltpu.VMEM((GROUPS, HD + ONES, LANES), f32),
            pltpu.VMEM((GROUPS, 1, LANES), f32),
            pltpu.VMEM((3, 2 * TOK, LANES), f32),
            pltpu.VMEM((3, 2 * TOK, LANES), f32),
            pltpu.VMEM((CHUNKS, CR, HEADS * HD), bf),
            pltpu.VMEM((HEADS * HD, OUT), bf),
            pltpu.VMEM((TOK, MINE), bf),
            pltpu.VMEM((CHUNKS, 2, CR, HALF), bf),
            pltpu.VMEM((CHUNKS, 2, CR, HALF), bf),
            pltpu.VMEM((CHUNKS, 4, CR, HALF), bf),
            pltpu.VMEM((CHUNKS, 4, CR, HALF), bf),
            dma((3,)),
            dma((4,)),
            dma((64,)),
            dma((5, NX, 2)),
            dma((2,)),
            dma((2,)),
            dma((CHUNKS, 6)),
            dma((CHUNKS, 6)),
            dma((CHUNKS,)),
        ],
        compiler_params=pltpu.CompilerParams(
            collective_id=0, has_side_effects=True, vmem_limit_bytes=60 << 20
        ),
        cost_estimate=pl.CostEstimate(flops=7 * 10**9, bytes_accessed=10**7, transcendentals=9 * 10**6),
    )(queries, keys, values, out_weight, doc_ids.reshape(1, TOK))


def solution(mesh):
    placed = (
        P(("dp", "ctx"), "tp"),
        P(("dp", "ctx"), "tp"),
        P(("dp", "ctx"), "tp"),
        P("tp", None),
        P(("dp", "ctx")),
    )
    return jax.shard_map(
        body, mesh=mesh, in_specs=placed, out_specs=P(("dp", "ctx"), "tp"), check_vma=False
    )
```

```python
import math

import jax
import jax.numpy as jnp
from jax import lax
from jax.experimental import pallas as pl
from jax.experimental.pallas import tpu as pltpu
from jax.sharding import PartitionSpec as P

MESH = pl.DeviceIdType.MESH
TOK = 256
HEADS = 8
HD = 128
NX = 4
NZ = 8
ROW = NX * TOK
OUT = 4096
MINE = 1024
HALF = MINE // 2
CHUNKS = 4
CR = TOK // CHUNKS
LANES = 256
SIDE = LANES // CR
PER = HEADS // SIDE
GROUPS = CHUNKS * PER
ONES = 16
LOG2E_SCALE = math.log2(math.e) / math.sqrt(HD)
NEG = -1e30
K, V = 0, 1
BOTH = ((K,), (V,))


def kernel(
    q_hbm, k_hbm, v_hbm, w_hbm, d_ref, out_hbm,
    qst, vst, qt, kb, vt, kx, vx, tk, tv, ok, ov, d2, acc, top, sa, sb, att, wv, out,
    snd_a, rcv_a, snd_n, rcv_n,
    lsem, wsem, gs, gr, tr, osem, ds, dr, osems,
):
    ctx = lax.axis_index("ctx")
    y = lax.axis_index("tp")
    z, x = ctx // NX, ctx % NX
    xp, xm, xo = (x + 1) % NX, (x + NX - 1) % NX, (x + 2) % NX
    dev_xp, dev_xm, dev_xo = z * NX + xp, z * NX + xm, z * NX + xo

    def plane(dz):
        return ((z + dz + NZ) % NZ) * NX + x

    dev_zp = plane(1)
    yp, ym, yo = (y + 1) % 4, (y + 3) % 4, (y + 2) % 4

    kcp = pltpu.make_async_copy(k_hbm, kb.at[0, x], lsem.at[0])
    vcp = pltpu.make_async_copy(v_hbm, vst, lsem.at[1])
    kcp.start()
    vcp.start()
    barrier = pltpu.get_barrier_semaphore()
    for dev in (dev_xp, dev_xm, dev_xo, plane(1), plane(-1), plane(2), plane(-2)):
        pl.semaphore_signal(barrier, inc=1, device_id={"ctx": dev}, device_id_type=MESH)
    for dev in (yp, ym):
        pl.semaphore_signal(barrier, inc=1, device_id={"tp": dev}, device_id_type=MESH)
    qcp = pltpu.make_async_copy(q_hbm, qst, lsem.at[2])
    qcp.start()
    vcp.wait()
    vt[0, x] = vst[...].T
    kcp.wait()
    pl.semaphore_wait(barrier, 9)

    pending = []

    def buf(row, col, what):
        if row == 4:
            return (kx, vx)[what]
        if row == 5:
            return (tk, tv)[what]
        if row == 6:
            return (ok, ov)[what]
        return (kb, vt)[what].at[row, col]

    def arrival(row, col, what):
        if row == 5:
            return tr.at[what]
        if row == 6:
            return osem.at[what]
        return gr.at[row, 0 if row == 4 else col, what]

    def send(src, dst, dev, whats=(K, V), when=None):
        for what in whats:
            cp = pltpu.make_async_remote_copy(
                src_ref=buf(*src, what),
                dst_ref=buf(*dst, what),
                send_sem=gs.at[len(pending)],
                recv_sem=arrival(*dst, what),
                device_id={"ctx": dev},
                device_id_type=MESH,
            )
            pending.append((cp, when))
            if when is None:
                cp.start()
            else:
                pl.when(when)(cp.start)

    def take(row, col, whats=(K, V), when=None):
        for what in whats:
            ref = buf(row, col, what)
            cp = pltpu.make_async_copy(ref, ref, arrival(row, col, what))
            if when is None:
                cp.wait()
            else:
                pl.when(when)(cp.wait)

    for w in BOTH:
        send((0, x), (1, x), dev_zp, w)
        send((0, x), (0, x), dev_xp, w, x < 3)
        send((0, x), (0, x), dev_xo, w, x < 2)
        send((0, x), (6, x), dev_xo, w, x >= 2)
        send((0, x), (5, x), plane(-2), w)
        send((0, x), (0, x), dev_xm, w, x == 0)

    for c in range(CHUNKS):
        d2[c] = jnp.concatenate([d_ref[:, c * CR : (c + 1) * CR]] * SIDE, axis=1)
    acc[...] = jnp.zeros_like(acc)
    top[...] = jnp.full_like(top, NEG)
    qcp.wait()
    for c in range(CHUNKS):
        for i in range(PER):
            heads = range(i * SIDE, (i + 1) * SIDE)
            part = [qst[c * CR : (c + 1) * CR, h * HD : (h + 1) * HD] for h in heads]
            qt[c * PER + i] = jnp.concatenate(part, axis=0).T

    def sides(row, w):
        send((row, x), (row, x), dev_xp, w)
        send((row, x), (row, x), dev_xm, w)

    key_row = lax.broadcasted_iota(jnp.int32, (TOK, LANES), 0)

    def sweep(blocks, lo, count, causal=False):
        hi = lo + count
        tiles = [blocks[i : i + 2] for i in range(0, len(blocks), 2)]

        def scores(g, dst, causal):
            first = d2[g // PER]
            high = None
            for j, tile in enumerate(tiles):
                s = jnp.dot(
                    jnp.concatenate([b[0][...] for b in tile], axis=0), qt[g],
                    preferred_element_type=jnp.float32,
                )
                pos = jnp.concatenate([key_row + b[2] for b in tile], axis=0)
                allowed = pos >= first
                if causal and j == 0:
                    lane = lax.broadcasted_iota(jnp.int32, (1, LANES), 1)
                    at = ctx * TOK + (g // PER) * CR + lane % CR
                    allowed = allowed & (pos <= at)
                s = jnp.where(allowed, s, NEG)
                dst[j, : s.shape[0]] = s
                part = jnp.max(s.reshape(s.shape[0] // 8, 8, LANES), axis=0)
                high = part if high is None else jnp.maximum(high, part)
            return high

        def absorb(g, src, high, nxt, more=True):
            old = top[g]
            new = jnp.maximum(old, jnp.max(high, axis=0, keepdims=True))
            top[g] = new
            factor = jnp.exp2((old - new) * LOG2E_SCALE)
            after = scores(g + 1, nxt, causal) if more else None
            total = None
            for j, tile in enumerate(tiles):
                n = len(tile) * TOK
                p = jnp.exp2((src[j, :n] - new) * LOG2E_SCALE).astype(jnp.bfloat16)
                values = jnp.concatenate([b[1][...] for b in tile], axis=1)
                values = jnp.concatenate([values, jnp.ones((ONES, n), jnp.bfloat16)], axis=0)
                part = jnp.dot(values, p, preferred_element_type=jnp.float32)
                total = part if total is None else total + part
            acc[g] = acc[g] * factor + total
            return after

        def two(t, high):
            g = lo + 2 * t
            high = absorb(g, sa, high, sb)
            return absorb(g + 1, sb, high, sa)

        high = scores(lo, sa, causal)
        if count > 2:
            high = lax.fori_loop(0, count // 2 - 1, two, high)
        absorb(hi - 1, sb, absorb(hi - 2, sa, high, sb), sa, more=False)

    def block(row, col, first):
        return (buf(row, col, K), buf(row, col, V), first)

    def far(row, col):
        return block(row, col, (z - row) * ROW + col * TOK)

    def mixed(col):
        return block(0, col, (z - jnp.where(col < x, 0, 4)) * ROW + col * TOK)

    for w in BOTH:
        take(1, x, w)
        send((1, x), (2, x), dev_zp, w)
        sides(1, w)
    for w in BOTH:
        take(5, x, w)
        send((5, x), (4, x), plane(-2), w)
    for w in BOTH:
        take(6, x, w, x < 2)
        send((6, x), (1, xo), dev_zp, w, x < 2)
        take(0, xo, w, x >= 2)
        send((0, xo), (1, xo), dev_zp, w, x >= 2)
    wcp = []
    for i in range(4):
        cp = pltpu.make_async_copy(w_hbm.at[pl.ds(i * 256, 256)], wv.at[pl.ds(i * 256, 256)], wsem.at[i])
        cp.start()
        wcp.append(cp)
    for w in BOTH:
        take(2, x, w)
        send((2, x), (3, x), dev_zp, w)
        sides(2, w)
    take(1, xp)
    take(1, xm)
    near = [block(0, x, ctx * TOK), far(1, x), far(1, xp), far(1, xm)]
    sweep(near, 0, GROUPS // 2, causal=True)
    for w in BOTH:
        take(1, xo, w)
        send((1, xo), (2, xo), dev_zp, w)
    for w in BOTH:
        take(4, x, w)
        send((4, x), (0, x), dev_xo, w, x > 1)
        send((4, x), (0, x), dev_xm, w, x > 0)
        send((4, x), (0, x), dev_xp, w, x == 3)
    sweep(near, GROUPS // 2, GROUPS // 2, causal=True)
    for w in BOTH:
        take(3, x, w)
        sides(3, w)
    sweep([far(1, xo), far(2, x), far(3, x), block(4, x, (z - 4) * ROW + x * TOK)], 0, GROUPS)
    for w in BOTH:
        take(2, xo, w)
        send((2, xo), (3, xo), dev_zp, w)
    take(2, xp)
    take(2, xm)
    take(0, xp)
    take(0, xm)
    sweep([far(2, xp), far(2, xm), mixed(xp), mixed(xm)], 0, GROUPS)
    sweep([far(2, xo)], 0, GROUPS)
    take(3, xp)
    take(3, xm)
    take(0, xo, when=x < 2)
    take(3, xo)
    for cp in wcp:
        cp.wait()

    def rs_copy(c, slot, src, dst, dev):
        return pltpu.make_async_remote_copy(
            src_ref=src,
            dst_ref=dst,
            send_sem=ds.at[c, slot],
            recv_sem=dr.at[c, slot],
            device_id={"tp": dev},
            device_id_type=MESH,
        )

    def copies(c):
        return (
            rs_copy(c, 0, snd_a.at[c, 0], rcv_a.at[c, 0], yp),
            rs_copy(c, 1, snd_a.at[c, 1], rcv_a.at[c, 1], ym),
            rs_copy(c, 2, snd_n.at[c, 0], rcv_n.at[c, 0], yp),
            rs_copy(c, 3, snd_n.at[c, 1], rcv_n.at[c, 1], ym),
            rs_copy(c, 4, snd_n.at[c, 2], rcv_n.at[c, 2], yp),
            rs_copy(c, 5, snd_n.at[c, 3], rcv_n.at[c, 3], ym),
        )

    def project(c, dest, half):
        cols = pl.ds(pl.multiple_of(dest * MINE + half * HALF, HALF), HALF)
        return jnp.dot(att[c], wv[:, cols], preferred_element_type=jnp.float32)

    def finish(c, carry):
        sweep([far(3, xp), far(3, xm), mixed(xo), far(3, xo)], c * PER, PER)
        for i in range(PER):
            a = acc[c * PER + i]
            o = (a[:HD] / a[HD : HD + 1]).T.astype(jnp.bfloat16)
            for side in range(SIDE):
                h = i * SIDE + side
                att[c, :, h * HD : (h + 1) * HD] = o[side * CR : (side + 1) * CR]
        cps = copies(c)
        for i, (dest, half, buffer, slot) in enumerate(
            ((yo, 0, snd_a, 0), (yo, 1, snd_a, 1), (yp, 1, snd_n, 0), (ym, 0, snd_n, 1))
        ):
            buffer[c, slot] = project(c, dest, half).astype(jnp.bfloat16)
            cps[i].start()
        return carry

    def relay(c, carry):
        cps = copies(c)
        for i, (dest, half) in enumerate(((yp, 0), (ym, 1))):
            part = project(c, dest, half)
            cps[i].wait_recv()
            snd_n[c, 2 + i] = (part + rcv_a[c, i].astype(jnp.float32)).astype(jnp.bfloat16)
            cps[4 + i].start()
        return carry

    def out_copy(c):
        rows = pl.ds(pl.multiple_of(c * CR, CR), CR)
        return pltpu.make_async_copy(out.at[rows], out_hbm.at[rows], osems.at[c])

    def collect(c, carry):
        cps = copies(c)
        own = [project(c, y, half) for half in (0, 1)]
        for i in range(2, 6):
            cps[i].wait_recv()
        rows = pl.ds(pl.multiple_of(c * CR, CR), CR)
        out[rows, :HALF] = (
            own[0] + rcv_n[c, 2].astype(jnp.float32) + rcv_n[c, 1].astype(jnp.float32)
        ).astype(jnp.bfloat16)
        out[rows, HALF:] = (
            own[1] + rcv_n[c, 0].astype(jnp.float32) + rcv_n[c, 3].astype(jnp.float32)
        ).astype(jnp.bfloat16)
        for cp in cps:
            cp.wait_send()
        out_copy(c).start()
        return carry

    lax.fori_loop(0, CHUNKS, finish, 0)
    lax.fori_loop(0, CHUNKS, relay, 0)
    lax.fori_loop(0, CHUNKS, collect, 0)
    for c in range(CHUNKS):
        out_copy(c).wait()
    for cp, when in pending:
        if when is None:
            cp.wait_send()
        else:
            pl.when(when)(cp.wait_send)


def body(queries, keys, values, out_weight, doc_ids):
    bf, f32 = jnp.bfloat16, jnp.float32
    hbm = pl.BlockSpec(memory_space=pltpu.HBM)
    vmem = pl.BlockSpec(memory_space=pltpu.VMEM)
    dma = pltpu.SemaphoreType.DMA
    return pl.pallas_call(
        kernel,
        out_shape=jax.ShapeDtypeStruct((TOK, MINE), bf),
        in_specs=[hbm] * 4 + [vmem],
        out_specs=hbm,
        scratch_shapes=[
            pltpu.VMEM((TOK, HEADS * HD), bf),
            pltpu.VMEM((TOK, HD), bf),
            pltpu.VMEM((GROUPS, HD, LANES), bf),
            pltpu.VMEM((4, NX, TOK, HD), bf),
            pltpu.VMEM((4, NX, HD, TOK), bf),
            pltpu.VMEM((TOK, HD), bf),
            pltpu.VMEM((HD, TOK), bf),
            pltpu.VMEM((TOK, HD), bf),
            pltpu.VMEM((HD, TOK), bf),
            pltpu.VMEM((TOK, HD), bf),
            pltpu.VMEM((HD, TOK), bf),
            pltpu.VMEM((CHUNKS, 1, LANES), jnp.int32),
            pltpu.VMEM((GROUPS, HD + ONES, LANES), f32),
            pltpu.VMEM((GROUPS, 1, LANES), f32),
            pltpu.VMEM((3, 2 * TOK, LANES), f32),
            pltpu.VMEM((3, 2 * TOK, LANES), f32),
            pltpu.VMEM((CHUNKS, CR, HEADS * HD), bf),
            pltpu.VMEM((HEADS * HD, OUT), bf),
            pltpu.VMEM((TOK, MINE), bf),
            pltpu.VMEM((CHUNKS, 2, CR, HALF), bf),
            pltpu.VMEM((CHUNKS, 2, CR, HALF), bf),
            pltpu.VMEM((CHUNKS, 4, CR, HALF), bf),
            pltpu.VMEM((CHUNKS, 4, CR, HALF), bf),
            dma((3,)),
            dma((4,)),
            dma((64,)),
            dma((5, NX, 2)),
            dma((2,)),
            dma((2,)),
            dma((CHUNKS, 6)),
            dma((CHUNKS, 6)),
            dma((CHUNKS,)),
        ],
        compiler_params=pltpu.CompilerParams(
            collective_id=0, has_side_effects=True, vmem_limit_bytes=60 << 20
        ),
        cost_estimate=pl.CostEstimate(flops=7 * 10**9, bytes_accessed=10**7, transcendentals=9 * 10**6),
    )(queries, keys, values, out_weight, doc_ids.reshape(1, TOK))


def solution(mesh):
    placed = (
        P(("dp", "ctx"), "tp"),
        P(("dp", "ctx"), "tp"),
        P(("dp", "ctx"), "tp"),
        P("tp", None),
        P(("dp", "ctx")),
    )
    return jax.shard_map(
        body, mesh=mesh, in_specs=placed, out_specs=P(("dp", "ctx"), "tp"), check_vma=False
    )
```
